512 devices in a mesh: blk: 32 (over x, y), layer: 16 (over z, core).
Axes of the slice: x: 4, y: 8, z: 8, core: 2. Of those that a mesh axis runs over, the one named last changes fastest.
Arguments:
- a_vals: float32 [16, 512, 6, 4096], P('layer', 'blk'), may hold values from -0.75 to 0.75
- a_cols: int32 [16, 512, 6], P('layer', 'blk'), may hold values from 0 to 31, all different within a row; in each aligned block of 16 rows (0 to 15, 16 to 31, ..., all dimensions but the last counted through in order) at most 6 rows name the same one
- b_vals: float32 [512, 4, 4096], P(('blk', 'layer')), may hold values from -6 to 6
- b_cols: int32 [512, 4], P(('blk', 'layer')), may hold values from 0 to 511, all different within a row
- c_cols: int32 [512, 16], P('blk'), may hold values from 0 to 511, all different within a row
- c_keep: int32 [512, 16], P('blk', 'layer'), may hold values 0 or 1
- c_vals: float32 [512, 16, 4096], P('blk', 'layer'), may hold values from -6 to 6
Outputs:
- x_next: float32 [512, 16, 4096], P('blk', 'layer')
The draws below stay inside these ranges and needn't reach their ends.
Inputs may be any that keep to these rules, and one draw needn't show every extreme that they name: `a_cols`: in each layer every block row names 6 different inner indices; of the 16 block rows of one device at most 6 name the same inner index in one layer, and some inner index is named by exactly 6 of them. `b_cols`: each block row names 4 different block columns. `c_cols`: each block row names 16 different block columns.
All inputs are finite; a program needn't handle non-finite values. No bound on the sum of `c_keep` on one device may be relied on, other than what follows from the above.
Results may differ from the reference program's by a relative error of at most 0.0003.
Values sent between devices are 32-bit elements; how exact they have to be, the bound alone decides.
A program may use at most 128 MiB of HBM per device.

```python
import math
import jax
import jax.numpy as jnp
import numpy as np
from jax import lax

BLK = 64
BB = 4096
BR = 1
RB = 16
NB = 512
NK = 32
CAP = 6
KAL = 6
KB = 4
MC = 16
TERMS = 1
N_LAYER = 16


def place_ends(result, own_key, least, top_value):
    longest = result.shape.index(max(result.shape))
    spots = []
    for shift in (0, 1):
        where = [jax.random.randint(jax.random.fold_in(own_key, axis), (), 0, length) for axis, length in enumerate(result.shape)]
        where[longest] = (where[longest] + shift) % result.shape[longest]
        spots.append(tuple(where))
    return result.at[spots[0]].set(least).at[spots[1]].set(top_value)


def block_levels(stream_key, shape, pieces, least, top_value):
    def one(dim, blocks):
        heights = jax.random.uniform(jax.random.fold_in(jax.random.fold_in(stream_key, 6), dim), (blocks,), jnp.float32, least / len(pieces), top_value / len(pieces))
        return jnp.repeat(jnp.exp(heights), shape[dim] // blocks).reshape((-1,) + (1,) * (len(shape) - dim - 1))

    factor_of = one(*pieces[0])
    for cut in pieces[1:]:
        factor_of = factor_of * one(*cut)
    return factor_of


def distinct(key, rows, count, top, lift):
    ranking = jax.random.permutation(jax.random.fold_in(key, 1), count)
    favour = ranking
    for power in range(3):
        favour = favour * favour // count
    favour = favour * lift // count
    lots = jax.random.randint(jax.random.fold_in(key, 2), (rows, count), 0, 4096) + favour
    holders = jax.random.permutation(jax.random.fold_in(key, 3), rows)[jnp.arange(count) % rows]
    lots = jnp.where(jnp.arange(rows)[:, None] == holders[None, :], 1 << 14, lots)
    priority = lots * count + jnp.arange(count)
    return lax.top_k(priority.astype(jnp.int32), top)[1].astype(jnp.int32)


def routed_block(rng, own, number, rows, amount, top, most, slope):
    order = jax.random.permutation(rng, amount)
    packed, usual = load_shares(amount, rows * top, most, slope, True), load_shares(amount, rows * top, most, slope, False)
    places = jnp.arange(amount)

    def named(tallies, rotation):
        used = int((tallies > 0).sum())
        fixed = max(1, used // 4)
        shifted = fixed + (places - fixed + rotation * (used - fixed)) % max(1, amount - fixed)
        return jnp.zeros((amount,), jnp.int32).at[order[jnp.where(places < fixed, places, shifted)]].set(jnp.asarray(tallies, jnp.int32))

    tallies = jnp.where(number % 4 == 0, named(packed, number // 4), named(usual, number - number // 4 - 1))
    mixed = jax.random.permutation(jax.random.fold_in(own, 3), amount)
    source_of, sink = mixed[0:amount // 2 * 2:2], mixed[1:amount // 2 * 2:2]
    margin = jnp.minimum(tallies[source_of] - 1, most - tallies[sink]) // 2
    margin = jnp.where((source_of == order[0]) | (sink == order[0]) | (tallies[sink] == 0), 0, jnp.maximum(margin, 0))
    shifted = jax.random.randint(jax.random.fold_in(own, 4), (amount // 2,), 0, 1 << 20) % (margin + 1)
    tallies = tallies.at[source_of].add(-shifted).at[sink].add(shifted)
    members = jnp.searchsorted(jnp.cumsum(tallies), jnp.arange(rows * top), side="right").astype(jnp.int32)
    grid = members.reshape(top, rows).T
    grid = grid[jax.random.permutation(jax.random.fold_in(own, 1), rows)]
    rotation = jax.random.randint(jax.random.fold_in(own, 2), (rows, 1), 0, top)
    return jnp.take_along_axis(grid, (jnp.arange(top)[None, :] + rotation) % top, axis=1)


def load_shares(number_of, total, reach, lean, full):
    weights = [(1 << 20) // math.isqrt(rank ** lean) + 1 for rank in range(1, number_of + 1)]
    largest = reach if full else min(reach, max(-(-total // number_of), total * weights[0] // sum(weights)))
    least = 1 if total - largest >= number_of - 1 else 0
    counts, surplus = [largest] + [least] * (number_of - 1), total - largest - least * (number_of - 1)
    while surplus > 0:
        movable = [i for i in range(1, number_of) if counts[i] < largest] or [i for i in range(1, number_of) if counts[i] < reach]
        pool, remaining = sum([weights[i] for i in movable]), surplus
        for i in movable:
            extra = min(reach - counts[i], max(1, remaining * weights[i] // pool), surplus)
            counts[i] = counts[i] + extra
            surplus = surplus - extra
    return np.array(counts)


def normal_values(own_key, shape, width, limit, pieces=(), kind=jnp.bfloat16):
    result = width * jax.random.normal(own_key, shape, jnp.float32)
    if pieces:
        result = result * block_levels(own_key, shape, pieces, -0.22, 0.18)
    return jnp.clip(result, -limit, limit).astype(kind)


def setup_inputs(seed: int = 0) -> dict:
    splits = jax.random.split(jax.random.key(seed), 8)
    a_vals = normal_values(splits[0], (N_LAYER, NB, KAL, BB), BLK ** -0.5, 0.75, ((0, 16), (1, 32)), jnp.float32)
    a_cols_keys = jax.random.split(jax.random.fold_in(splits[1], 1), N_LAYER * NB // RB)
    a_cols_turns = jax.random.permutation(jax.random.fold_in(splits[1], 3), N_LAYER * NB // RB)
    a_cols = jax.vmap(lambda own, number: routed_block(jax.random.fold_in(splits[1], 2), own, number, RB, NK, KAL, CAP, 2))(a_cols_keys, a_cols_turns).reshape((N_LAYER, NB, KAL))
    b_vals = normal_values(splits[2], (NB, KB, BB), TERMS ** -0.5, 6.0, ((0, 512),), jnp.float32)
    b_cols = distinct(splits[3], NB, NB, KB, 0)
    c_cols = distinct(splits[4], NB, NB, MC, 0)
    c_keep = place_ends((jax.random.randint(splits[5], (NB, MC), 0, 4) < 3).astype(jnp.int32), jax.random.fold_in(splits[5], 1), 0, 1)
    c_vals = normal_values(splits[6], (NB, MC, BB), 1.0, 6.0, ((0, 32), (1, 16)), jnp.float32)
    return {"a_vals": a_vals, "a_cols": a_cols, "b_vals": b_vals, "b_cols": b_cols, "c_cols": c_cols, "c_keep": c_keep, "c_vals": c_vals}


def reference(a_vals, a_cols, b_vals, b_cols, c_cols, c_keep, c_vals):
    layer_ids = jnp.arange(N_LAYER, dtype=jnp.int32)[:, None, None]
    inner_rows = ((a_cols // BR) * N_LAYER + layer_ids) * BR + a_cols % BR
    left_rows = jnp.transpose(a_vals, (1, 0, 2, 3)).reshape(NB, N_LAYER * KAL, BLK, BLK)
    inner_lists = jnp.transpose(inner_rows, (1, 0, 2)).reshape(NB, N_LAYER * KAL)
    right_blocks = b_vals.reshape(NB, KB, BLK, BLK)

    def one_row(inputs):
        left, inner, targets = inputs
        chosen = right_blocks[inner]
        landing = b_cols[inner]
        products = jnp.einsum("sxy,skyz->skxz", left, chosen, precision=lax.Precision.HIGHEST)
        agrees = (landing[:, :, None] == targets[None, None, :]).astype(jnp.float32)
        return jnp.einsum("skm,skxz->mxz", agrees, products, precision=lax.Precision.HIGHEST)

    product = lax.map(one_row, (left_rows, inner_lists, c_cols)).reshape(NB, MC, BB)
    keep = c_keep.astype(jnp.float32)[:, :, None]
    return keep * (1.5 * c_vals - 0.5 * product)
```

```python
import functools

import jax
import jax.numpy as jnp
from jax import lax
from jax.experimental import pallas as pl
from jax.experimental.pallas import tpu as pltpu
from jax.sharding import PartitionSpec as P

NX, NY, NZ = 4, 8, 8
CAP = 6
MESH = pl.DeviceIdType.MESH
F32, BF16, I32 = jnp.float32, jnp.bfloat16, jnp.int32
EXACT = lax.Precision.HIGHEST


def kernel(
    a_ref, acol_ref, b_ref, bcol_ref, ccol_ref, out_ref,
    g0, g1, ap, prod, tab, tab_s, off, off_s, core_out, core_in, z_in,
    loc_sem, ag_send, ag_recv, core_send, core_recv, z_send, z_recv,
):
    rows, per_row = 16, 6
    n_inner = NX * NY
    per_k = 4 * CAP
    zero_block = n_inner * per_k
    me, lay = lax.axis_index("blk"), lax.axis_index("layer")
    x, y = me // NY, me % NY
    z, c = lay // 2, lay % 2

    def blk_of(dx, dy):
        return (x + dx + NX) % NX * NY + (y + dy + NY) % NY

    def layer_of(dz):
        return (z + dz + NZ) % NZ * 2 + c

    sibling = z * 2 + 1 - c
    x_step = {0: (1, 0), 1: (-1, 0), 2: (0, 1), 3: (0, -1)}

    barrier = pltpu.get_barrier_semaphore()
    for d in range(4):
        pl.semaphore_signal(barrier, inc=1, device_id=(blk_of(*x_step[d]), lay), device_id_type=MESH)
    for other in (sibling, layer_of(1), layer_of(-1)):
        pl.semaphore_signal(barrier, inc=1, device_id=(me, other), device_id_type=MESH)

    lane = lax.broadcasted_iota(I32, (32, 128), 1)
    low = lane < 64

    for pair in range(2):
        first = b_ref[pl.ds(2 * pair, 32, stride=4), :]
        second = b_ref[pl.ds(2 * pair + 1, 32, stride=4), :]
        even = jnp.where(low, first, pltpu.roll(second, 64, 1))
        odd = jnp.where(low, pltpu.roll(first, 64, 1), second)
        g = g0 if pair == 0 else g1
        g[me, pl.ds(0, 32, stride=2), :] = even
        g[me, pl.ds(1, 32, stride=2), :] = odd
    sub8 = lax.broadcasted_iota(I32, (8, 128), 0)
    meta = jnp.full((8, 128), -1, I32)
    for s in range(4):
        meta = jnp.where(sub8 == s, bcol_ref[0, s], meta)
    g0[me, 64:72, :] = meta.astype(F32)

    pl.semaphore_wait(barrier, 7)

    def ag_copy(half, k, d):
        buf = g0 if half == 0 else g1
        return pltpu.make_async_remote_copy(
            src_ref=buf.at[k], dst_ref=buf.at[k],
            send_sem=ag_send.at[half, d, k], recv_sem=ag_recv.at[half, k],
            device_id=(blk_of(*x_step[d]), lay), device_id_type=MESH,
        )

    def act(half, k, d, what):
        copy = ag_copy(half, k, d)
        if what == "start":
            copy.start()
        else:
            copy.wait_send()

    def y_sends(half, dx, dy, what):
        k = blk_of(dx, dy)
        even = (x + dx + NX) % 2 == 0
        if -2 <= dy <= 0:
            act(half, k, 2, what)
        if 0 <= dy <= 2:
            act(half, k, 3, what)
        if dy == -3:
            pl.when(even)(lambda: act(half, k, 2, what))
        if dy == 3:
            pl.when(jnp.logical_not(even))(lambda: act(half, k, 3, what))

    def x_sends(half, dx, dy, what):
        k = blk_of(dx, dy)
        even = (y + dy + NY) % 2 == 0
        if dx == 0:
            act(half, k, 0, what)
            act(half, k, 1, what)
        if dx == -1:
            pl.when(even)(lambda: act(half, k, 0, what))
        if dx == 1:
            pl.when(jnp.logical_not(even))(lambda: act(half, k, 1, what))

    def arrive(half, dx, dy):
        ag_copy(half, blk_of(dx, dy), 0).wait_recv()

    x_sends(0, 0, 0, "start")
    y_sends(1, 0, 0, "start")
    x_sends(1, 0, 0, "start")
    y_sends(0, 0, 0, "start")

    tile = (lax.broadcasted_iota(I32, (rows, 128), 1) % rows == lax.broadcasted_iota(I32, (rows, 128), 0)).astype(F32)
    spread = jnp.dot(acol_ref[...].astype(F32), tile, preferred_element_type=F32, precision=EXACT)
    lane6 = lax.broadcasted_iota(I32, (per_row, 128), 1)
    mine6 = lane6 // rows == lax.broadcasted_iota(I32, (per_row, 128), 0)
    a_lane = jnp.sum(jnp.where(mine6, spread, 0.0), axis=0, keepdims=True)
    lane1 = lax.broadcasted_iota(I32, (1, 128), 1)
    a_lane = jnp.where(lane1 < rows * per_row, a_lane, -1.0)
    inner = lax.broadcasted_iota(I32, (n_inner, 128), 0).astype(F32)
    onehot = (inner == a_lane).astype(F32)
    before = (lax.broadcasted_iota(I32, (128, 128), 0) < lax.broadcasted_iota(I32, (128, 128), 1)).astype(F32)
    count = jnp.dot(onehot, before, preferred_element_type=F32, precision=EXACT)
    rank = jnp.sum(onehot * count, axis=0, keepdims=True)
    table = jnp.zeros((n_inner, 128), F32)
    lane_f = lane.astype(F32)
    for r in range(CAP):
        hit = jnp.where(count == float(r), onehot, 0.0)
        table = jnp.where(lane == r, jnp.sum(hit * lane_f, axis=1, keepdims=True), table)
    tab[...] = jnp.clip(table.astype(I32), 0, rows * per_row - 1)
    tab_copy = pltpu.make_async_copy(tab, tab_s, loc_sem.at[0])
    tab_copy.start()

    def prepare(n, carry):
        a, i = n // rows, n % rows
        block = a_ref[a, i // 8, pl.ds(i % 8, 32, stride=8), :]
        high = block.astype(BF16).astype(F32)
        rest = block - high
        ap[n, 0:32, :] = jnp.where(low, high, pltpu.roll(rest, 64, 1)).astype(BF16)
        ap[n, 32:64, :] = jnp.where(low, pltpu.roll(high, 64, 1), rest).astype(BF16)
        return carry

    lax.fori_loop(0, rows * per_row, prepare, 0)
    prod[zero_block] = jnp.zeros((32, 128), F32)
    tab_copy.wait()

    def products(k):
        right = jnp.concatenate([g0[k, 0:64, :], g1[k]], axis=1)
        high = right.astype(BF16)
        rest = (right - high.astype(F32)).astype(BF16)
        weights = jnp.concatenate([high, high, rest, rest], axis=0)
        left = jnp.concatenate([ap[tab_s[k, r]] for r in range(CAP)], axis=0)
        left = jnp.concatenate([left, left], axis=1)
        both = jnp.dot(left, weights, preferred_element_type=F32)
        for r in range(CAP):
            for pair in range(2):
                even = both[r * 64:r * 64 + 32, pair * 128:pair * 128 + 128]
                odd = both[r * 64 + 32:r * 64 + 64, pair * 128:pair * 128 + 128]
                prod[k * per_k + 2 * pair * CAP + r] = jnp.where(low, even, pltpu.roll(odd, 64, 1))
                prod[k * per_k + (2 * pair + 1) * CAP + r] = jnp.where(low, pltpu.roll(even, 64, 1), odd)

    def stage_dys(h):
        return [0] if h == 0 else ([4] if h == 4 else [-h, h])

    def stage_products(h):
        dys = stage_dys(h)

        def one(u, carry):
            dy = h if len(dys) == 1 else h * (2 * (u // NX) - 1)
            products((x + u) % NX * NY + (y + dy + NY) % NY)
            return carry

        lax.fori_loop(0, NX * len(dys), one, 0)

    for h in range(7):
        if h == 0:
            for dx in (-1, 1, 2):
                arrive(0, dx, 0)
                x_sends(0, dx, 0, "start")
                y_sends(0, dx, 0, "start")
        elif h <= 4:
            for dy in stage_dys(h):
                arrive(1, 0, dy)
                y_sends(1, 0, dy, "start")
                x_sends(1, 0, dy, "start")
                for dx in (0, -1, 1, 2):
                    arrive(0, dx, dy)
                    y_sends(0, dx, dy, "start")
        if 1 <= h <= 5:
            for dy in stage_dys(h - 1):
                for dx in (-1, 1):
                    arrive(1, dx, dy)
                    x_sends(1, dx, dy, "start")
        if h >= 2:
            for dy in stage_dys(h - 2):
                arrive(1, 2, dy)
            stage_products(h - 2)

    target = lax.dot_general(ccol_ref[...].astype(F32), tile, (((0,), (0,)), ((), ())), preferred_element_type=F32, precision=EXACT)

    def pick(k, cols):
        return jnp.where(a_lane == k.astype(F32), g0[k, 64:72, :], cols)

    cols = lax.fori_loop(0, n_inner, pick, jnp.full((8, 128), -1.0, F32))
    base = a_lane * float(per_k) + rank
    where_from = jnp.full((rows, 128), float(zero_block), F32)
    for s in range(4):
        where_from = jnp.where(target == cols[s:s + 1, :], base + float(CAP * s), where_from)
    off[...] = jnp.clip(where_from.astype(I32), 0, zero_block)
    off_copy = pltpu.make_async_copy(off, off_s, loc_sem.at[1])
    off_copy.start()
    off_copy.wait()

    def landed(m, i):
        total = prod[off_s[m, i]]
        for a in range(1, per_row):
            total = total + prod[off_s[m, a * rows + i]]
        return total

    def core_copy(part, delta):
        slot = part * NZ + delta % NZ
        return pltpu.make_async_remote_copy(
            src_ref=core_out.at[slot], dst_ref=core_in.at[slot],
            send_sem=core_send.at[slot], recv_sem=core_recv.at[slot],
            device_id=(me, sibling), device_id_type=MESH,
        )

    def give(part, delta):
        slot = part * NZ + delta % NZ
        m = (z + delta + NZ) % NZ * 2 + 1 - c

        def one(i, carry):
            core_out[slot, i] = landed(m, part * 8 + i)
            return carry

        lax.fori_loop(0, 8, one, 0)
        core_copy(part, delta).start()

    def z_copy(way, part, t):
        slot = (way * 2 + part) * 4 + t - 1
        source = core_in.at[part * NZ + z_delta(way, part, t) % NZ]
        return pltpu.make_async_remote_copy(
            src_ref=source, dst_ref=z_in.at[slot],
            send_sem=z_send.at[slot], recv_sem=z_recv.at[slot],
            device_id=(me, layer_of(1 - 2 * way)), device_id_type=MESH,
        )

    def z_steps(way, part):
        return 4 if way == part else 3

    def z_delta(way, part, t):
        return (z_steps(way, part) + 1 - t) * (1 - 2 * way)

    def pass_on(way, part, t):
        delta = z_delta(way, part, t)
        slot = part * NZ + delta % NZ
        m = (z + delta + NZ) % NZ * 2 + c
        core_copy(part, delta).wait_recv()
        if t > 1:
            z_copy(way, part, t - 1).wait_recv()

        def one(i, carry):
            total = landed(m, part * 8 + i) + core_in[slot, i]
            if t > 1:
                total = total + z_in[(way * 2 + part) * 4 + t - 2, i]
            core_in[slot, i] = total
            return carry

        lax.fori_loop(0, 8, one, 0)
        z_copy(way, part, t).start()

    def pieces(t):
        return [(way, part) for way, part in ((0, 0), (1, 1), (0, 1), (1, 0)) if t <= z_steps(way, part)]

    def give_all(t):
        if t <= 4:
            for way, part in pieces(t):
                give(part, z_delta(way, part, t))
        else:
            give(0, 0)
            give(1, 0)

    give_all(1)
    for t in range(1, 5):
        give_all(t + 1)
        for way, part in pieces(t):
            pass_on(way, part, t)

    for part in range(2):
        core_copy(part, 0).wait_recv()
        for way in range(2):
            z_copy(way, part, z_steps(way, part)).wait_recv()

        def one(i, carry):
            total = landed(z * 2 + c, part * 8 + i) + core_in[part * NZ, i]
            for way in range(2):
                total = total + z_in[(way * 2 + part) * 4 + z_steps(way, part) - 1, i]
            out_ref[part * 8 + i] = total
            return carry

        lax.fori_loop(0, 8, one, 0)

    for h in range(5):
        for dy in stage_dys(h):
            for dx in (0, -1, 1, 2):
                y_sends(0, dx, dy, "wait")
                x_sends(1, dx, dy, "wait")
            y_sends(1, 0, dy, "wait")
    for dx in (0, -1, 1):
        x_sends(0, dx, 0, "wait")
    for part in range(2):
        for delta in range(NZ):
            core_copy(part, delta).wait_send()
    for t in range(1, 5):
        for way, part in pieces(t):
            z_copy(way, part, t).wait_send()


def body(a_vals, a_cols, b_vals, b_cols, c_cols, c_keep, c_vals):
    n_inner = NX * NY
    a = jnp.transpose(a_vals[0], (1, 0, 2)).reshape(6, 2, 8, 32, 128)
    a = jnp.transpose(a, (0, 1, 3, 2, 4)).reshape(6, 2, 256, 128)
    b = jnp.transpose(b_vals[0].reshape(4, 32, 128), (1, 0, 2)).reshape(128, 128)
    vmem = pl.BlockSpec(memory_space=pltpu.VMEM)
    smem = pl.BlockSpec(memory_space=pltpu.SMEM)
    dma = pltpu.SemaphoreType.DMA
    summed = pl.pallas_call(
        kernel,
        out_shape=jax.ShapeDtypeStruct((16, 32, 128), F32),
        in_specs=[vmem, vmem, vmem, smem, vmem],
        out_specs=vmem,
        scratch_shapes=[
            pltpu.VMEM((n_inner, 72, 128), F32),
            pltpu.VMEM((n_inner, 64, 128), F32),
            pltpu.VMEM((96, 64, 128), BF16),
            pltpu.VMEM((n_inner * 4 * CAP + 1, 32, 128), F32),
            pltpu.VMEM((n_inner, 128), I32),
            pltpu.SMEM((n_inner, 128), I32),
            pltpu.VMEM((16, 128), I32),
            pltpu.SMEM((16, 128), I32),
            pltpu.VMEM((16, 8, 32, 128), F32),
            pltpu.VMEM((16, 8, 32, 128), F32),
            pltpu.VMEM((16, 8, 32, 128), F32),
            dma((2,)),
            dma((2, 4, n_inner)),
            dma((2, n_inner)),
            dma((16,)),
            dma((16,)),
            dma((16,)),
            dma((16,)),
        ],
        compiler_params=pltpu.CompilerParams(
            collective_id=0, has_side_effects=True, vmem_limit_bytes=48 << 20
        ),
        cost_estimate=pl.CostEstimate(flops=1 << 31, bytes_accessed=8 << 20, transcendentals=0),
    )(a, a_cols[0].T, b, b_cols, c_cols)
    keep = c_keep.astype(F32)[:, :, None]
    return keep * (1.5 * c_vals - 0.5 * summed.reshape(16, 1, 4096))


def solution(mesh):
    in_specs = (
        P("layer", "blk", None, None),
        P("layer", "blk", None),
        P(("blk", "layer"), None, None),
        P(("blk", "layer"), None),
        P("blk", None),
        P("blk", "layer"),
        P("blk", "layer", None),
    )
    out_specs = P("blk", "layer", None)
    return jax.shard_map(body, mesh=mesh, in_specs=in_specs, out_specs=out_specs, check_vma=False)
```

```python
import jax
import jax.numpy as jnp
from jax import lax
from jax.experimental import pallas as pl
from jax.experimental.pallas import tpu as pltpu
from jax.sharding import PartitionSpec as P

NX, NY, NZ = 4, 8, 8
CAP = 6
MESH = pl.DeviceIdType.MESH
F32, BF16, I32 = jnp.float32, jnp.bfloat16, jnp.int32
EXACT = lax.Precision.HIGHEST


def kernel(
    a_hbm, acol_hbm, b_hbm, bcol_hbm, ccol_hbm, keep_hbm, cval_hbm, out_ref,
    a_ref, acol_ref, b_ref, bcol_ref, ccol_ref, keep_ref, cval_ref,
    g0, g1, ap, prod, tab, tab_s, off, off_s, core_out, core_in, z_in,
    loc_sem, ag_send, ag_recv, core_send, core_recv, z_send, z_recv,
):
    rows, per_row = 16, 6
    n_inner = NX * NY
    per_k = 4 * CAP
    zero_block = n_inner * per_k
    me, lay = lax.axis_index("blk"), lax.axis_index("layer")
    x, y = me // NY, me % NY
    z, c = lay // 2, lay % 2
    sibling = z * 2 + 1 - c

    def blk_of(dx, dy):
        return (x + dx + NX) % NX * NY + (y + dy + NY) % NY

    def layer_of(dz):
        return (z + dz + NZ) % NZ * 2 + c

    loads = [
        pltpu.make_async_copy(src, dst, loc_sem.at[n])
        for n, (src, dst) in enumerate((
            (b_hbm, b_ref), (bcol_hbm, bcol_ref), (acol_hbm, acol_ref), (ccol_hbm, ccol_ref),
            (keep_hbm, keep_ref), (a_hbm, a_ref), (cval_hbm, cval_ref),
        ))
    ]
    for load in loads:
        load.start()

    steps = ((1, 0), (-1, 0), (0, 1), (0, -1))
    barrier = pltpu.get_barrier_semaphore()
    for step in steps:
        pl.semaphore_signal(barrier, inc=1, device_id=(blk_of(*step), lay), device_id_type=MESH)
    for other in (sibling, layer_of(1), layer_of(-1)):
        pl.semaphore_signal(barrier, inc=1, device_id=(me, other), device_id_type=MESH)

    lane = lax.broadcasted_iota(I32, (32, 128), 1)
    low = lane < 64

    loads[0].wait()
    for pair in range(2):
        first = b_ref[pl.ds(2 * pair, 32, stride=4), :]
        second = b_ref[pl.ds(2 * pair + 1, 32, stride=4), :]
        even = jnp.where(low, first, pltpu.roll(second, 64, 1))
        odd = jnp.where(low, pltpu.roll(first, 64, 1), second)
        g = g0 if pair == 0 else g1
        g[me, pl.ds(0, 32, stride=2), :] = even
        g[me, pl.ds(1, 32, stride=2), :] = odd
    loads[1].wait()
    sub8 = lax.broadcasted_iota(I32, (8, 128), 0)
    meta = jnp.full((8, 128), -1, I32)
    for s in range(4):
        meta = jnp.where(sub8 == s, bcol_ref[0, s], meta)
    g0[me, 64:72, :] = meta.astype(F32)

    pl.semaphore_wait(barrier, 7)

    def ag_copy(half, k, d):
        buf = g0 if half == 0 else g1
        return pltpu.make_async_remote_copy(
            src_ref=buf.at[k], dst_ref=buf.at[k],
            send_sem=ag_send.at[half, d, k], recv_sem=ag_recv.at[half, k],
            device_id=(blk_of(*steps[d]), lay), device_id_type=MESH,
        )

    def act(half, k, d, start):
        if start:
            ag_copy(half, k, d).start()
        else:
            ag_copy(half, k, d).wait_send()

    def arrive(half, dx, dy):
        ag_copy(half, blk_of(dx, dy), 0).wait_recv()

    def send_all(half, k, ds, start):
        for d in ds:
            act(half, k, d, start)

    def y_on(half, dx, h, side, start):
        goes = (h <= 2) | ((h == 3) & ((x + dx) % 2 == side))
        k = blk_of(dx, h * (2 * side - 1))
        pl.when(goes)(lambda: act(half, k, 2 + side, start))

    def x_on(half, dy, start):
        even = (y + dy + NY) % 2 == 0
        pl.when(even)(lambda: act(half, blk_of(-1, dy), 0, start))
        pl.when(jnp.logical_not(even))(lambda: act(half, blk_of(1, dy), 1, start))

    send_all(0, me, (0, 1), True)
    send_all(1, me, (2, 3, 0, 1), True)
    send_all(0, me, (2, 3), True)

    tile = (lax.broadcasted_iota(I32, (rows, 128), 1) % rows == lax.broadcasted_iota(I32, (rows, 128), 0)).astype(F32)
    loads[2].wait()
    acol = jnp.concatenate([acol_ref[a] for a in range(per_row)], axis=0)
    spread = jnp.dot(acol.astype(F32), tile, preferred_element_type=F32, precision=EXACT)
    lane6 = lax.broadcasted_iota(I32, (per_row, 128), 1)
    mine6 = lane6 // rows == lax.broadcasted_iota(I32, (per_row, 128), 0)
    a_lane = jnp.sum(jnp.where(mine6, spread, 0.0), axis=0, keepdims=True)
    lane1 = lax.broadcasted_iota(I32, (1, 128), 1)
    a_lane = jnp.where(lane1 < rows * per_row, a_lane, -1.0)
    inner = lax.broadcasted_iota(I32, (n_inner, 128), 0).astype(F32)
    onehot = (inner == a_lane).astype(F32)
    before = (lax.broadcasted_iota(I32, (128, 128), 0) < lax.broadcasted_iota(I32, (128, 128), 1)).astype(BF16)
    count = jnp.dot(onehot.astype(BF16), before, preferred_element_type=F32)

    for dx in (1, -1):
        arrive(0, dx, 0)
        send_all(0, blk_of(dx, 0), (2, 3), True)
    x_on(0, 0, True)

    rank = jnp.sum(onehot * count, axis=0, keepdims=True)
    table = jnp.zeros((n_inner, 128), F32)
    lane_f = lane.astype(F32)
    for r in range(CAP):
        hit = jnp.where(count == float(r), onehot, 0.0)
        table = jnp.where(lane == r, jnp.sum(hit * lane_f, axis=1, keepdims=True), table)
    tab[...] = jnp.clip(table.astype(I32), 0, rows * per_row - 1)
    tab_copy = pltpu.make_async_copy(tab, tab_s, loc_sem.at[7])
    tab_copy.start()
    loads[3].wait()
    target = lax.dot_general(ccol_ref[...].astype(F32), tile, (((0,), (0,)), ((), ())), preferred_element_type=F32, precision=EXACT)
    prod[zero_block] = jnp.zeros((32, 128), F32)
    loads[5].wait()

    arrive(0, 2, 0)
    send_all(0, blk_of(2, 0), (2, 3), True)
    tab_copy.wait()

    def prepare(n, carry):
        a, i = n // rows, n % rows
        block = a_ref[a, i // 8, pl.ds(i % 8, 32, stride=8), :]
        high = block.astype(BF16).astype(F32)
        rest = block - high
        ap[n, 0:32, :] = jnp.where(low, high, pltpu.roll(rest, 64, 1)).astype(BF16)
        ap[n, 32:64, :] = jnp.where(low, pltpu.roll(high, 64, 1), rest).astype(BF16)
        return carry

    def products(k):
        right = jnp.concatenate([g0[k, 0:64, :], g1[k]], axis=1)
        high = right.astype(BF16)
        rest = (right - high.astype(F32)).astype(BF16)
        weights = jnp.concatenate([high, high, rest, rest], axis=0)
        left = jnp.concatenate([ap[tab_s[k, r]] for r in range(CAP)], axis=0)
        left = jnp.concatenate([left, left], axis=1)
        both = jnp.dot(left, weights, preferred_element_type=F32)
        for r in range(CAP):
            for pair in range(2):
                even = both[r * 64:r * 64 + 32, pair * 128:pair * 128 + 128]
                odd = both[r * 64 + 32:r * 64 + 64, pair * 128:pair * 128 + 128]
                prod[k * per_k + 2 * pair * CAP + r] = jnp.where(low, even, pltpu.roll(odd, 64, 1))
                prod[k * per_k + (2 * pair + 1) * CAP + r] = jnp.where(low, pltpu.roll(even, 64, 1), odd)

    def find_sources():
        def pick(k, cols):
            return jnp.where(a_lane == k.astype(F32), g0[k, 64:72, :], cols)

        cols = lax.fori_loop(0, n_inner, pick, jnp.full((8, 128), -1.0, F32), unroll=8)
        base = a_lane * float(per_k) + rank
        where_from = jnp.full((rows, 128), float(zero_block), F32)
        for s in range(4):
            where_from = jnp.where(target == cols[s:s + 1, :], base + float(CAP * s), where_from)
        off[...] = jnp.clip(where_from.astype(I32), 0, zero_block)
        pltpu.make_async_copy(off, off_s, loc_sem.at[8]).start()

    def gather_step(n, carry):
        h, u = n // NX + 1, n % NX
        dx = u + (u // 2) * (5 - 2 * u)
        older = (-(h - 1), (h - 1) * (1 - h // 5))
        pl.when(n == 4 * NX)(find_sources)

        for side in range(2):
            dy = h * (2 * side - 1)

            @pl.when(h <= 4 - side)
            def _():
                @pl.when(u == 0)
                def _():
                    arrive(1, 0, dy)
                    y_on(1, 0, h, side, True)
                    send_all(1, blk_of(0, dy), (0, 1), True)

                arrive(0, dx, dy)
                y_on(0, dx, h, side, True)

        for side in range(2):
            @pl.when((u == 0) & ((side == 0) | ((h >= 2) & (h <= 4))))
            def _():
                arrive(1, 1, older[side])
                arrive(1, -1, older[side])
                x_on(1, older[side], True)

        @pl.when(h == 1)
        def _():
            lax.fori_loop(0, 24, lambda j, carry: prepare(u * 24 + j, carry), 0, unroll=4)

        @pl.when(h >= 2)
        def _():
            @pl.when(u == 3)
            def _():
                for side in range(2):
                    arrive(1, 2, older[side])

            for side in range(2):
                products(blk_of(dx, older[side]))

        return carry

    lax.fori_loop(0, 5 * NX, gather_step, 0)
    pltpu.make_async_copy(off, off_s, loc_sem.at[8]).wait()

    def landed(m, i):
        total = prod[off_s[m, i]]
        for a in range(1, per_row):
            total = total + prod[off_s[m, a * rows + i]]
        return total

    def core_copy(part, delta):
        slot = part * NZ + delta % NZ
        return pltpu.make_async_remote_copy(
            src_ref=core_out.at[slot], dst_ref=core_in.at[slot],
            send_sem=core_send.at[slot], recv_sem=core_recv.at[slot],
            device_id=(me, sibling), device_id_type=MESH,
        )

    def give(part, delta):
        slot = part * NZ + delta % NZ
        m = (z + delta + NZ) % NZ * 2 + 1 - c

        def one(i, carry):
            core_out[slot, i] = landed(m, part * 8 + i)
            return carry

        lax.fori_loop(0, 8, one, 0, unroll=4)
        core_copy(part, delta).start()

    def z_copy(way, part, t):
        slot = (way * 2 + part) * 4 + t - 1
        source = core_in.at[part * NZ + z_delta(way, part, t) % NZ]
        return pltpu.make_async_remote_copy(
            src_ref=source, dst_ref=z_in.at[slot],
            send_sem=z_send.at[slot], recv_sem=z_recv.at[slot],
            device_id=(me, layer_of(1 - 2 * way)), device_id_type=MESH,
        )

    def z_steps(way, part):
        return 4 if way == part else 3

    def z_delta(way, part, t):
        return (z_steps(way, part) + 1 - t) * (1 - 2 * way)

    def pass_on(way, part, t):
        delta = z_delta(way, part, t)
        slot = part * NZ + delta % NZ
        m = (z + delta + NZ) % NZ * 2 + c
        core_copy(part, delta).wait_recv()
        if t > 1:
            z_copy(way, part, t - 1).wait_recv()

        def one(i, carry):
            total = landed(m, part * 8 + i) + core_in[slot, i]
            if t > 1:
                total = total + z_in[(way * 2 + part) * 4 + t - 2, i]
            core_in[slot, i] = total
            return carry

        lax.fori_loop(0, 8, one, 0, unroll=4)
        z_copy(way, part, t).start()

    def pieces(t):
        return [(way, part) for way, part in ((0, 0), (1, 1), (0, 1), (1, 0)) if t <= z_steps(way, part)]

    def give_all(t):
        if t <= 4:
            for way, part in pieces(t):
                give(part, z_delta(way, part, t))
        else:
            give(0, 0)
            give(1, 0)

    give_all(1)
    for t in range(1, 5):
        for way, part in pieces(t):
            pass_on(way, part, t)
        give_all(t + 1)

    loads[4].wait()
    loads[6].wait()
    for part in range(2):
        core_copy(part, 0).wait_recv()
        for way in range(2):
            z_copy(way, part, z_steps(way, part)).wait_recv()

        def one(n, carry):
            i = part * 8 + n
            total = landed(z * 2 + c, i) + core_in[part * NZ, n]
            for way in range(2):
                total = total + z_in[(way * 2 + part) * 4 + z_steps(way, part) - 1, n]
            out_ref[i] = keep_ref[0, i].astype(F32) * (1.5 * cval_ref[i] - 0.5 * total)
            return carry

        lax.fori_loop(0, 8, one, 0, unroll=4)

    send_all(0, me, (0, 1), False)
    x_on(0, 0, False)
    send_all(1, me, (2, 3, 0, 1), False)
    x_on(1, 0, False)
    for dx in range(NX):
        send_all(0, blk_of(dx, 0), (2, 3), False)

    def left(n, carry):
        h, u = n // NX + 1, n % NX
        for side in range(2):
            @pl.when(h <= 4 - side)
            def _():
                y_on(0, u, h, side, False)

                @pl.when(u == 0)
                def _():
                    y_on(1, 0, h, side, False)
                    send_all(1, blk_of(0, h * (2 * side - 1)), (0, 1), False)
                    x_on(1, h * (2 * side - 1), False)

        return carry

    lax.fori_loop(0, 4 * NX, left, 0)
    for part in range(2):
        for delta in range(NZ):
            core_copy(part, delta).wait_send()
    for t in range(1, 5):
        for way, part in pieces(t):
            z_copy(way, part, t).wait_send()


def body(a_vals, a_cols, b_vals, b_cols, c_cols, c_keep, c_vals):
    n_inner = NX * NY
    a = jnp.transpose(a_vals[0], (1, 0, 2)).reshape(6, 2, 8, 32, 128)
    a = jnp.transpose(a, (0, 1, 3, 2, 4)).reshape(6, 2, 256, 128)
    b = jnp.transpose(b_vals[0].reshape(4, 32, 128), (1, 0, 2)).reshape(128, 128)
    acol = jnp.transpose(a_cols, (2, 0, 1))
    hbm = pl.BlockSpec(memory_space=pltpu.HBM)
    vmem, smem, dma = pltpu.VMEM, pltpu.SMEM, pltpu.SemaphoreType.DMA
    out = pl.pallas_call(
        kernel,
        out_shape=jax.ShapeDtypeStruct((16, 32, 128), F32),
        in_specs=[hbm] * 7,
        out_specs=pl.BlockSpec(memory_space=pltpu.VMEM),
        scratch_shapes=[
            vmem((6, 2, 256, 128), F32),
            vmem((6, 1, 16), I32),
            vmem((128, 128), F32),
            smem((1, 4), I32),
            vmem((16, 16), I32),
            smem((1, 16), I32),
            vmem((16, 32, 128), F32),
            vmem((n_inner, 72, 128), F32),
            vmem((n_inner, 64, 128), F32),
            vmem((96, 64, 128), BF16),
            vmem((n_inner * 4 * CAP + 1, 32, 128), F32),
            vmem((n_inner, 128), I32),
            smem((n_inner, 128), I32),
            vmem((16, 128), I32),
            smem((16, 128), I32),
            vmem((16, 8, 32, 128), F32),
            vmem((16, 8, 32, 128), F32),
            vmem((16, 8, 32, 128), F32),
            dma((9,)),
            dma((2, 4, n_inner)),
            dma((2, n_inner)),
            dma((16,)),
            dma((16,)),
            dma((16,)),
            dma((16,)),
        ],
        compiler_params=pltpu.CompilerParams(
            collective_id=0, has_side_effects=True, vmem_limit_bytes=(64 << 20) - (64 << 10)
        ),
        cost_estimate=pl.CostEstimate(flops=1 << 31, bytes_accessed=8 << 20, transcendentals=0),
    )(a, acol, b, b_cols, c_cols, c_keep.T, c_vals.reshape(16, 32, 128))
    return out.reshape(16, 1, 4096)


def solution(mesh):
    in_specs = (
        P("layer", "blk", None, None),
        P("layer", "blk", None),
        P(("blk", "layer"), None, None),
        P(("blk", "layer"), None),
        P("blk", None),
        P("blk", "layer"),
        P("blk", "layer", None),
    )
    out_specs = P("blk", "layer", None)
    return jax.shard_map(body, mesh=mesh, in_specs=in_specs, out_specs=out_specs, check_vma=False)
```

```python
import jax
import jax.numpy as jnp
from jax import lax
from jax.experimental import pallas as pl
from jax.experimental.pallas import tpu as pltpu
from jax.sharding import PartitionSpec as P

NX, NY, NZ = 4, 8, 8
SPLIT = 40
CAP = 6
MESH = pl.DeviceIdType.MESH
F32, BF16, I32 = jnp.float32, jnp.bfloat16, jnp.int32
EXACT = lax.Precision.HIGHEST


def kernel(
    a_hbm, acol_hbm, b_hbm, bcol_hbm, ccol_hbm, keep_hbm, cval_hbm, out_ref,
    a_ref, acol_ref, b_ref, bcol_ref, ccol_ref, keep_ref, cval_ref,
    g, ap, prod, tab, tab_s, off, off_s, core_out, core_in, z_in,
    loc_sem, ag_send, ag_recv, core_send, core_recv, z_send, z_recv,
):
    rows, per_row = 16, 6
    n_inner = NX * NY
    per_k = 4 * CAP
    zero_block = n_inner * per_k
    me, lay = lax.axis_index("blk"), lax.axis_index("layer")
    x, y = me // NY, me % NY
    z, c = lay // 2, lay % 2
    sibling = z * 2 + 1 - c

    def blk_of(dx, dy):
        return (x + dx + NX) % NX * NY + (y + dy + NY) % NY

    def layer_of(dz):
        return (z + dz + NZ) % NZ * 2 + c

    loads = [
        pltpu.make_async_copy(src, dst, loc_sem.at[n])
        for n, (src, dst) in enumerate((
            (b_hbm, b_ref), (bcol_hbm, bcol_ref), (acol_hbm, acol_ref), (ccol_hbm, ccol_ref),
            (keep_hbm, keep_ref), (a_hbm, a_ref), (cval_hbm, cval_ref),
        ))
    ]
    for load in loads:
        load.start()

    steps = ((1, 0), (-1, 0), (0, 1), (0, -1))
    barrier = pltpu.get_barrier_semaphore()
    for step in steps:
        pl.semaphore_signal(barrier, inc=1, device_id=(blk_of(*step), lay), device_id_type=MESH)
    for other in (sibling, layer_of(1), layer_of(-1)):
        pl.semaphore_signal(barrier, inc=1, device_id=(me, other), device_id_type=MESH)

    lane = lax.broadcasted_iota(I32, (32, 128), 1)
    low = lane < 64

    loads[0].wait()
    quarter = lane // 32
    blocks = [b_ref[pl.ds(s, 32, stride=4), :] for s in range(4)]
    for q in range(2):
        for parity in range(2):
            lines = blocks[0]
            for s in range(4):
                by = (s - 2 * parity - q) % 4 * 32
                moved = pltpu.roll(blocks[s], by, 1) if by else blocks[s]
                lines = moved if s == 0 else jnp.where(quarter == s, moved, lines)
            g[q, me, pl.ds(parity, 32, stride=2), :] = lines
    loads[1].wait()
    sub8 = lax.broadcasted_iota(I32, (8, 128), 0)
    meta = jnp.full((8, 128), -1, I32)
    for s in range(4):
        meta = jnp.where(sub8 == s, bcol_ref[0, s], meta)
    g[0, me, 64:72, :] = meta.astype(F32)

    pl.semaphore_wait(barrier, 7)

    def ag_copy(q, half, k, d):
        lines = pl.ds(0, SPLIT) if half == 1 else pl.ds(SPLIT, (72 if q == 0 else 64) - SPLIT)
        return pltpu.make_async_remote_copy(
            src_ref=g.at[q, k, lines], dst_ref=g.at[q, k, lines],
            send_sem=ag_send.at[q, half, d, k], recv_sem=ag_recv.at[q, half, k],
            device_id=(blk_of(*steps[d]), lay), device_id_type=MESH,
        )

    def act(q, half, k, d, start):
        if start:
            ag_copy(q, half, k, d).start()
        else:
            ag_copy(q, half, k, d).wait_send()

    def arrive(q, half, dx, dy):
        ag_copy(q, half, blk_of(dx, dy), 0).wait_recv()

    def send_all(q, half, k, ds, start):
        for d in ds:
            act(q, half, k, d, start)

    def y_on(q, half, dx, h, side, start):
        goes = (h <= 2) | ((h == 3) & ((x + dx) % 2 == side))
        k = blk_of(dx, h * (2 * side - 1))
        pl.when(goes)(lambda: act(q, half, k, 2 + side, start))

    def x_on(q, half, dy, start):
        even = (y + dy + NY) % 2 == 0
        pl.when(even)(lambda: act(q, half, blk_of(-1, dy), 0, start))
        pl.when(jnp.logical_not(even))(lambda: act(q, half, blk_of(1, dy), 1, start))

    def own(q, start):
        send_all(q, 0, me, (0, 1), start)
        send_all(q, 1, me, (2, 3, 0, 1), start)
        send_all(q, 0, me, (2, 3), start)

    def near(q):
        for dx in (1, -1):
            arrive(q, 0, dx, 0)
            send_all(q, 0, blk_of(dx, 0), (2, 3), True)
        x_on(q, 0, 0, True)

    def opposite(q):
        arrive(q, 0, 2, 0)
        send_all(q, 0, blk_of(2, 0), (2, 3), True)

    own(0, True)

    tile = (lax.broadcasted_iota(I32, (rows, 128), 1) % rows == lax.broadcasted_iota(I32, (rows, 128), 0)).astype(F32)
    loads[2].wait()
    acol = jnp.concatenate([acol_ref[a] for a in range(per_row)], axis=0)
    spread = jnp.dot(acol.astype(F32), tile, preferred_element_type=F32, precision=EXACT)
    lane6 = lax.broadcasted_iota(I32, (per_row, 128), 1)
    mine6 = lane6 // rows == lax.broadcasted_iota(I32, (per_row, 128), 0)
    a_lane = jnp.sum(jnp.where(mine6, spread, 0.0), axis=0, keepdims=True)
    lane1 = lax.broadcasted_iota(I32, (1, 128), 1)
    a_lane = jnp.where(lane1 < rows * per_row, a_lane, -1.0)
    inner = lax.broadcasted_iota(I32, (n_inner, 128), 0).astype(F32)
    onehot = (inner == a_lane).astype(F32)
    before = (lax.broadcasted_iota(I32, (128, 128), 0) < lax.broadcasted_iota(I32, (128, 128), 1)).astype(BF16)
    count = jnp.dot(onehot.astype(BF16), before, preferred_element_type=F32)

    near(0)

    rank = jnp.sum(onehot * count, axis=0, keepdims=True)
    table = jnp.zeros((n_inner, 128), F32)
    lane_f = lane.astype(F32)
    for r in range(CAP):
        hit = jnp.where(count == float(r), onehot, 0.0)
        table = jnp.where(lane == r, jnp.sum(hit * lane_f, axis=1, keepdims=True), table)
    tab[...] = jnp.clip(table.astype(I32), 0, rows * per_row - 1)
    tab_copy = pltpu.make_async_copy(tab, tab_s, loc_sem.at[7])
    tab_copy.start()
    loads[3].wait()
    target = lax.dot_general(ccol_ref[...].astype(F32), tile, (((0,), (0,)), ((), ())), preferred_element_type=F32, precision=EXACT)
    for q in range(2):
        prod[q, zero_block] = jnp.zeros((16, 128), F32)
    loads[5].wait()

    opposite(0)
    tab_copy.wait()

    def prepare(n, carry):
        a, i = n // rows, n % rows
        block = a_ref[a, i // 8, pl.ds(i % 8, 32, stride=8), :]
        high = block.astype(BF16).astype(F32)
        rest = block - high
        ap[n, 0:32, :] = jnp.where(low, high, pltpu.roll(rest, 64, 1)).astype(BF16)
        ap[n, 32:64, :] = jnp.where(low, pltpu.roll(high, 64, 1), rest).astype(BF16)
        return carry

    quarter16 = lax.broadcasted_iota(I32, (16, 128), 1) // 32

    def exchange(one, other, width):
        even = quarter16 // width % 2 == 0
        return (
            jnp.where(even, one, pltpu.roll(other, 32 * width, 1)),
            jnp.where(even, pltpu.roll(one, 128 - 32 * width, 1), other),
        )

    def products(q, k):
        right = g[q, k, 0:64, :]
        high = right.astype(BF16)
        rest = (right - high.astype(F32)).astype(BF16)
        weights = jnp.concatenate([high, high, rest, rest], axis=0)
        left = jnp.concatenate([ap[tab_s[k, r]] for r in range(CAP)], axis=0)
        left = jnp.concatenate([left, left], axis=1)
        both = jnp.dot(left, weights, preferred_element_type=F32)
        for r in range(CAP):
            w = [both[r * 64 + e * 16:r * 64 + e * 16 + 16, :] for e in range(4)]
            w[0], w[1] = exchange(w[0], w[1], 1)
            w[2], w[3] = exchange(w[2], w[3], 1)
            w[0], w[2] = exchange(w[0], w[2], 2)
            w[1], w[3] = exchange(w[1], w[3], 2)
            for s in range(4):
                prod[q, k * per_k + s * CAP + r] = w[s]

    def find_sources():
        def pick(k, cols):
            return jnp.where(a_lane == k.astype(F32), g[0, k, 64:72, :], cols)

        cols = lax.fori_loop(0, n_inner, pick, jnp.full((8, 128), -1.0, F32), unroll=8)
        base = a_lane * float(per_k) + rank
        where_from = jnp.full((rows, 128), float(zero_block), F32)
        for s in range(4):
            where_from = jnp.where(target == cols[s:s + 1, :], base + float(CAP * s), where_from)
        off[...] = jnp.clip(where_from.astype(I32), 0, zero_block)
        pltpu.make_async_copy(off, off_s, loc_sem.at[8]).start()

    def order(u):
        return u + (u // 2) * (5 - 2 * u)

    def gather_step(q, h, u):
        dx = order(u)
        older = (1 - h, h - 1)

        for side in range(2):
            dy = h * (2 * side - 1)

            @pl.when(h <= 4 - side)
            def _():
                @pl.when(u == 0)
                def _():
                    arrive(q, 1, 0, dy)
                    y_on(q, 1, 0, h, side, True)
                    send_all(q, 1, blk_of(0, dy), (0, 1), True)

                arrive(q, 0, dx, dy)
                y_on(q, 0, dx, h, side, True)

        for side in range(2):
            @pl.when((u == 0) & (h >= 1 + side))
            def _():
                arrive(q, 1, 1, older[side])
                arrive(q, 1, -1, older[side])
                x_on(q, 1, older[side], True)

        @pl.when(h >= 2)
        def _():
            @pl.when(u == 3)
            def _():
                for side in range(2):
                    arrive(q, 1, 2, older[side])

            for side in range(2):
                products(q, blk_of(dx, older[side]))

    def last_step(q, u):
        @pl.when(u == 0)
        def _():
            arrive(q, 1, 1, -4)
            arrive(q, 1, -1, -4)
            x_on(q, 1, -4, True)

        @pl.when(u == 3)
        def _():
            arrive(q, 1, 2, -4)
            arrive(q, 1, 2, 0)

        for dy in (-4, 0):
            products(q, blk_of(order(u), dy))

    def landed(q, m, i):
        total = prod[q, off_s[m, i]]
        for a in range(1, per_row):
            total = total + prod[q, off_s[m, a * rows + i]]
        return total

    def core_copy(q, part, delta):
        slot = part * NZ + delta % NZ
        return pltpu.make_async_remote_copy(
            src_ref=core_out.at[q, slot], dst_ref=core_in.at[q, slot],
            send_sem=core_send.at[q, slot], recv_sem=core_recv.at[q, slot],
            device_id=(me, sibling), device_id_type=MESH,
        )

    def give(q, part, delta):
        slot = part * NZ + delta % NZ
        m = (z + delta + NZ) % NZ * 2 + 1 - c

        def one(i, carry):
            core_out[q, slot, i] = landed(q, m, part * 8 + i)
            return carry

        lax.fori_loop(0, 8, one, 0, unroll=4)
        core_copy(q, part, delta).start()

    def z_copy(q, way, part, t):
        slot = (way * 2 + part) * 4 + t - 1
        source = core_in.at[q, part * NZ + z_delta(way, part, t) % NZ]
        return pltpu.make_async_remote_copy(
            src_ref=source, dst_ref=z_in.at[q, slot],
            send_sem=z_send.at[q, slot], recv_sem=z_recv.at[q, slot],
            device_id=(me, layer_of(1 - 2 * way)), device_id_type=MESH,
        )

    def z_steps(way, part):
        return 4 if way == part else 3

    def z_delta(way, part, t):
        return (z_steps(way, part) + 1 - t) * (1 - 2 * way)

    def pass_on(q, way, part, t):
        delta = z_delta(way, part, t)
        slot = part * NZ + delta % NZ
        m = (z + delta + NZ) % NZ * 2 + c
        core_copy(q, part, delta).wait_recv()
        if t > 1:
            z_copy(q, way, part, t - 1).wait_recv()

        def one(i, carry):
            total = landed(q, m, part * 8 + i) + core_in[q, slot, i]
            if t > 1:
                total = total + z_in[q, (way * 2 + part) * 4 + t - 2, i]
            core_in[q, slot, i] = total
            return carry

        lax.fori_loop(0, 8, one, 0, unroll=4)
        z_copy(q, way, part, t).start()

    def pieces(t):
        return [(way, part) for way, part in ((0, 0), (1, 1), (0, 1), (1, 0)) if t <= z_steps(way, part)]

    def give_all(q, t):
        if t <= 4:
            for way, part in pieces(t):
                give(q, part, z_delta(way, part, t))
        if t == 4:
            give(q, 0, 0)
            give(q, 1, 0)

    def pass_all(q, t, which):
        for way, part in pieces(t)[which]:
            pass_on(q, way, part, t)

    first, second = slice(0, 2), slice(2, 4)

    def gather_0(n, carry):
        h, u = n // NX + 1, n % NX

        @pl.when(h == 1)
        def _():
            lax.fori_loop(0, 24, lambda j, t: prepare(u * 24 + j, t), 0, unroll=4)

        gather_step(0, h, u)
        pl.when(n == 10)(lambda: own(1, True))
        pl.when(n == 13)(lambda: near(1))
        pl.when(n == 15)(lambda: opposite(1))
        return carry

    lax.fori_loop(0, 4 * NX, gather_0, 0)
    find_sources()

    def gather_1(n, carry):
        h, u = n // NX + 1, n % NX
        gather_step(1, h, u)
        pl.when(h == 1)(lambda: last_step(0, u))

        @pl.when(n == 4)
        def _():
            pltpu.make_async_copy(off, off_s, loc_sem.at[8]).wait()
            give_all(0, 1)

        pl.when(n == 5)(lambda: give_all(0, 2))
        pl.when(n == 6)(lambda: pass_all(0, 1, first))
        pl.when(n == 7)(lambda: pass_all(0, 1, second))
        pl.when(n == 8)(lambda: give_all(0, 3))
        pl.when(n == 10)(lambda: pass_all(0, 2, first))
        pl.when(n == 11)(lambda: pass_all(0, 2, second))
        pl.when(n == 12)(lambda: give_all(0, 4))
        pl.when(n == 14)(lambda: pass_all(0, 3, first))
        pl.when(n == 15)(lambda: pass_all(0, 3, second))
        return carry

    lax.fori_loop(0, 4 * NX, gather_1, 0)

    def finish_1(u, carry):
        last_step(1, u)
        return carry

    lax.fori_loop(0, NX, finish_1, 0)
    give_all(1, 1)
    pass_all(0, 4, first)
    for t in range(1, 5):
        give_all(1, t + 1)
        pass_all(1, t, slice(0, 4))

    loads[4].wait()
    loads[6].wait()
    for part in range(2):
        for q in range(2):
            core_copy(q, part, 0).wait_recv()
            for way in range(2):
                z_copy(q, way, part, z_steps(way, part)).wait_recv()

        def one(n, carry):
            i = part * 8 + n
            half = []
            for q in range(2):
                total = landed(q, z * 2 + c, i) + core_in[q, part * NZ, n]
                for way in range(2):
                    total = total + z_in[q, (way * 2 + part) * 4 + z_steps(way, part) - 1, n]
                half.append(total)
            keep = keep_ref[0, i].astype(F32)
            for lines, total in zip((pl.ds(0, 16), pl.ds(16, 16)), exchange(half[0], half[1], 1)):
                out_ref[i, lines, :] = keep * (1.5 * cval_ref[i, lines, :] - 0.5 * total)
            return carry

        lax.fori_loop(0, 8, one, 0, unroll=4)

    def left(n, carry):
        h, u = n // NX + 1, n % NX
        for q in range(2):
            for side in range(2):
                @pl.when(h <= 4 - side)
                def _():
                    y_on(q, 0, u, h, side, False)

                    @pl.when(u == 0)
                    def _():
                        dy = h * (2 * side - 1)
                        y_on(q, 1, 0, h, side, False)
                        send_all(q, 1, blk_of(0, dy), (0, 1), False)
                        x_on(q, 1, dy, False)

        return carry

    lax.fori_loop(0, 4 * NX, left, 0)
    for q in range(2):
        own(q, False)
        x_on(q, 0, 0, False)
        x_on(q, 1, 0, False)
        for dx in range(1, NX):
            send_all(q, 0, blk_of(dx, 0), (2, 3), False)
        for part in range(2):
            for delta in range(NZ):
                core_copy(q, part, delta).wait_send()
        for t in range(1, 5):
            for way, part in pieces(t):
                z_copy(q, way, part, t).wait_send()


def body(a_vals, a_cols, b_vals, b_cols, c_cols, c_keep, c_vals):
    n_inner = NX * NY
    a = jnp.transpose(a_vals[0], (1, 0, 2)).reshape(6, 2, 8, 32, 128)
    a = jnp.transpose(a, (0, 1, 3, 2, 4)).reshape(6, 2, 256, 128)
    b = jnp.transpose(b_vals[0].reshape(4, 32, 128), (1, 0, 2)).reshape(128, 128)
    acol = jnp.transpose(a_cols, (2, 0, 1))
    hbm = pl.BlockSpec(memory_space=pltpu.HBM)
    vmem, smem, dma = pltpu.VMEM, pltpu.SMEM, pltpu.SemaphoreType.DMA
    out = pl.pallas_call(
        kernel,
        out_shape=jax.ShapeDtypeStruct((16, 32, 128), F32),
        in_specs=[hbm] * 7,
        out_specs=pl.BlockSpec(memory_space=pltpu.VMEM),
        scratch_shapes=[
            vmem((6, 2, 256, 128), F32),
            vmem((6, 1, 16), I32),
            vmem((128, 128), F32),
            smem((1, 4), I32),
            vmem((16, 16), I32),
            smem((1, 16), I32),
            vmem((16, 32, 128), F32),
            vmem((2, n_inner, 72, 128), F32),
            vmem((96, 64, 128), BF16),
            vmem((2, n_inner * 4 * CAP + 1, 16, 128), F32),
            vmem((n_inner, 128), I32),
            smem((n_inner, 128), I32),
            vmem((16, 128), I32),
            smem((16, 128), I32),
            vmem((2, 16, 8, 16, 128), F32),
            vmem((2, 16, 8, 16, 128), F32),
            vmem((2, 16, 8, 16, 128), F32),
            dma((9,)),
            dma((2, 2, 4, n_inner)),
            dma((2, 2, n_inner)),
            dma((2, 16)),
            dma((2, 16)),
            dma((2, 16)),
            dma((2, 16)),
        ],
        compiler_params=pltpu.CompilerParams(
            collective_id=0, has_side_effects=True, vmem_limit_bytes=(64 << 20) - (64 << 10)
        ),
        cost_estimate=pl.CostEstimate(flops=1 << 31, bytes_accessed=8 << 20, transcendentals=0),
    )(a, acol, b, b_cols, c_cols, c_keep.T, c_vals.reshape(16, 32, 128))
    return out.reshape(16, 1, 4096)


def solution(mesh):
    in_specs = (
        P("layer", "blk", None, None),
        P("layer", "blk", None),
        P(("blk", "layer"), None, None),
        P(("blk", "layer"), None),
        P("blk", None),
        P("blk", "layer"),
        P("blk", "layer", None),
    )
    out_specs = P("blk", "layer", None)
    return jax.shard_map(body, mesh=mesh, in_specs=in_specs, out_specs=out_specs, check_vma=False)
```

```python
import jax
import jax.numpy as jnp
from jax import lax
from jax.experimental import pallas as pl
from jax.experimental.pallas import tpu as pltpu
from jax.sharding import PartitionSpec as P

NX, NY, NZ = 4, 8, 8
CAP = 6
MESH = pl.DeviceIdType.MESH
F32, BF16, I32 = jnp.float32, jnp.bfloat16, jnp.int32
EXACT = lax.Precision.HIGHEST


def kernel(
    a_hbm, acol_hbm, b_hbm, bcol_hbm, ccol_hbm, keep_hbm, cval_hbm, out_ref,
    a_ref, acol_ref, b_ref, bcol_ref, ccol_ref, keep_ref, cval_ref,
    g0, g1, ap, prod, tab, tab_s, off, off_s, core_out, core_in, z_in,
    loc_sem, ag_send, g0_recv, g1_recv, core_send, core_recv, z_send, z_recv,
):
    rows, per_row = 16, 6
    n_inner = NX * NY
    per_k = 4 * CAP
    zero_block = n_inner * per_k
    me, lay = lax.axis_index("blk"), lax.axis_index("layer")
    x, y = me // NY, me % NY
    z, c = lay // 2, lay % 2
    sibling = z * 2 + 1 - c

    def blk_of(dx, dy):
        return (x + dx + NX) % NX * NY + (y + dy + NY) % NY

    def layer_of(dz):
        return (z + dz + NZ) % NZ * 2 + c

    loads = [
        pltpu.make_async_copy(src, dst, loc_sem.at[n])
        for n, (src, dst) in enumerate((
            (b_hbm, b_ref), (bcol_hbm, bcol_ref), (acol_hbm, acol_ref), (ccol_hbm, ccol_ref),
            (keep_hbm, keep_ref), (a_hbm, a_ref), (cval_hbm, cval_ref),
        ))
    ]
    for load in loads:
        load.start()

    steps = ((1, 0), (-1, 0), (0, 1), (0, -1))
    barrier = pltpu.get_barrier_semaphore()
    for step in steps:
        pl.semaphore_signal(barrier, inc=1, device_id=(blk_of(*step), lay), device_id_type=MESH)
    for other in (sibling, layer_of(1), layer_of(-1)):
        pl.semaphore_signal(barrier, inc=1, device_id=(me, other), device_id_type=MESH)

    lane = lax.broadcasted_iota(I32, (32, 128), 1)
    low = lane < 64

    loads[0].wait()
    for pair in range(2):
        first = b_ref[pl.ds(2 * pair, 32, stride=4), :]
        second = b_ref[pl.ds(2 * pair + 1, 32, stride=4), :]
        even = jnp.where(low, first, pltpu.roll(second, 64, 1))
        odd = jnp.where(low, pltpu.roll(first, 64, 1), second)
        g = g0 if pair == 0 else g1
        g[0, pl.ds(0, 32, stride=2), :] = even
        g[0, pl.ds(1, 32, stride=2), :] = odd
    loads[1].wait()
    sub8 = lax.broadcasted_iota(I32, (8, 128), 0)
    meta = jnp.full((8, 128), -1, I32)
    for s in range(4):
        meta = jnp.where(sub8 == s, bcol_ref[0, s], meta)
    g0[0, 64:72, :] = meta.astype(F32)

    pl.semaphore_wait(barrier, 7)

    def send(buf, recv, n, src, dst, d, count, lines=slice(None)):
        lines = pl.ds(*lines) if isinstance(lines, tuple) else lines
        pltpu.make_async_remote_copy(
            src_ref=buf.at[pl.ds(src, count), lines], dst_ref=buf.at[pl.ds(dst, count), lines],
            send_sem=ag_send.at[0 if buf is g0 else 1], recv_sem=recv.at[n],
            device_id=(blk_of(*steps[d]), lay), device_id_type=MESH,
        ).start()

    def arrive(buf, recv, n, place, count, lines=slice(None)):
        lines = pl.ds(*lines) if isinstance(lines, tuple) else lines
        piece = buf.at[pl.ds(place, count), lines]
        pltpu.make_async_copy(piece, piece, recv.at[n]).wait()

    def row0_on(part):
        src, count = ((0, 3), (3, 1))[part]
        for side in range(2):
            send(g0, g0_recv, 4 + 2 * (1 + side) + part, src, (1 + side) * NX + src, 2 + side, count)

    def x_pair(yi, count):
        for d in range(2):
            send(g1, g1_recv, 16 + 8 * (1 - d) + yi, yi, (2 - d) * NY + yi, d, count)

    def x_on(xi, yi):
        send(g1, g1_recv, 32 + yi, xi * NY + yi, 3 * NY + yi, 2 - xi, 1)

    for d in range(2):
        send(g0, g0_recv, 1 - d, 0, 2 - d, d, 1)
    for side in range(2):
        send(g1, g1_recv, 1 + side, 0, 1 + side, 2 + side, 1)
    x_pair(0, 1)

    tile = (lax.broadcasted_iota(I32, (rows, 128), 1) % rows == lax.broadcasted_iota(I32, (rows, 128), 0)).astype(F32)
    loads[2].wait()
    acol = jnp.concatenate([acol_ref[a] for a in range(per_row)], axis=0)
    spread = jnp.dot(acol.astype(F32), tile, preferred_element_type=F32, precision=EXACT)
    lane6 = lax.broadcasted_iota(I32, (per_row, 128), 1)
    mine6 = lane6 // rows == lax.broadcasted_iota(I32, (per_row, 128), 0)
    a_lane = jnp.sum(jnp.where(mine6, spread, 0.0), axis=0, keepdims=True)
    lane1 = lax.broadcasted_iota(I32, (1, 128), 1)
    a_lane = jnp.where(lane1 < rows * per_row, a_lane, -1.0)
    inner = lax.broadcasted_iota(I32, (n_inner, 128), 0).astype(F32)
    onehot = (inner == a_lane).astype(F32)
    before = (lax.broadcasted_iota(I32, (128, 128), 0) < lax.broadcasted_iota(I32, (128, 128), 1)).astype(BF16)
    count = jnp.dot(onehot.astype(BF16), before, preferred_element_type=F32)

    for xi in (1, 2):
        arrive(g0, g0_recv, xi - 1, xi, 1)
    send(g0, g0_recv, 2, 2, 3, 0, 1)
    row0_on(0)

    rank = jnp.sum(onehot * count, axis=0, keepdims=True)
    table = jnp.zeros((n_inner, 128), F32)
    lane_f = lane.astype(F32)
    for r in range(CAP):
        hit = jnp.where(count == float(r), onehot, 0.0)
        table = jnp.where(lane == r, jnp.sum(hit * lane_f, axis=1, keepdims=True), table)
    tab[...] = jnp.clip(table.astype(I32), 0, rows * per_row - 1)
    tab_copy = pltpu.make_async_copy(tab, tab_s, loc_sem.at[7])
    tab_copy.start()
    loads[3].wait()
    target = lax.dot_general(ccol_ref[...].astype(F32), tile, (((0,), (0,)), ((), ())), preferred_element_type=F32, precision=EXACT)
    prod[zero_block] = jnp.zeros((32, 128), F32)
    loads[5].wait()

    arrive(g0, g0_recv, 2, 3, 1)
    row0_on(1)
    tab_copy.wait()

    def prepare(n, carry):
        a, i = n // rows, n % rows
        block = a_ref[a, i // 8, pl.ds(i % 8, 32, stride=8), :]
        high = block.astype(BF16).astype(F32)
        rest = block - high
        ap[n, 0:32, :] = jnp.where(low, high, pltpu.roll(rest, 64, 1)).astype(BF16)
        ap[n, 32:64, :] = jnp.where(low, pltpu.roll(high, 64, 1), rest).astype(BF16)
        return carry

    def inner_at(xi, yi):
        dx = xi + xi // 2 * (5 - 2 * xi)
        dy = (yi + 1) // 2 * (1 - 2 * (yi % 2))
        return (x + dx) % NX * NY + (y + dy + NY) % NY

    def products(xi, yi):
        k = inner_at(xi, yi)
        right = jnp.concatenate([g0[yi * NX + xi, 0:64, :], g1[xi * NY + yi]], axis=1)
        high = right.astype(BF16)
        rest = (right - high.astype(F32)).astype(BF16)
        weights = jnp.concatenate([high, high, rest, rest], axis=0)
        left = jnp.concatenate([ap[tab_s[k, r]] for r in range(CAP)], axis=0)
        left = jnp.concatenate([left, left], axis=1)
        both = jnp.dot(left, weights, preferred_element_type=F32)
        for r in range(CAP):
            for pair in range(2):
                even = both[r * 64:r * 64 + 32, pair * 128:pair * 128 + 128]
                odd = both[r * 64 + 32:r * 64 + 64, pair * 128:pair * 128 + 128]
                prod[k * per_k + 2 * pair * CAP + r] = jnp.where(low, even, pltpu.roll(odd, 64, 1))
                prod[k * per_k + (2 * pair + 1) * CAP + r] = jnp.where(low, pltpu.roll(even, 64, 1), odd)

    def find_sources():
        def pick(k, cols):
            return jnp.where(a_lane == inner_at(k % NX, k // NX).astype(F32), g0[k, 64:72, :], cols)

        cols = lax.fori_loop(0, n_inner, pick, jnp.full((8, 128), -1.0, F32), unroll=8)
        base = a_lane * float(per_k) + rank
        where_from = jnp.full((rows, 128), float(zero_block), F32)
        for s in range(4):
            where_from = jnp.where(target == cols[s:s + 1, :], base + float(CAP * s), where_from)
        off[...] = jnp.clip(where_from.astype(I32), 0, zero_block)
        pltpu.make_async_copy(off, off_s, loc_sem.at[8]).start()

    def gather_step(h, carry):
        early, late = 2 * h - 1, 2 * h

        @pl.when(h <= 3)
        def _():
            for side, yi in ((0, early), (1, late)):
                arrive(g1, g1_recv, yi, yi, 1)

                @pl.when(h <= 2)
                def _():
                    send(g1, g1_recv, yi + 2, yi, yi + 2, 2 + side, 1)

                @pl.when(h == 3)
                def _():
                    send(g1, g1_recv, 7 + side, yi, 7, 2 + side, 1, (32 * side, 32))

            x_pair(early, 2)
            for side, yi in ((0, early), (1, late)):
                @pl.when(h == 1)
                def _():
                    arrive(g0, g0_recv, 4 + 2 * yi, yi * NX, 3)
                    arrive(g0, g0_recv, 5 + 2 * yi, yi * NX + 3, 1)

                @pl.when(h >= 2)
                def _():
                    arrive(g0, g0_recv, 4 + 2 * yi, yi * NX, NX)

                @pl.when(h <= 2)
                def _():
                    send(g0, g0_recv, 8 + 2 * yi, yi * NX, (yi + 2) * NX, 2 + side, NX)

                @pl.when(h == 3)
                def _():
                    send(g0, g0_recv, 18 + side, yi * NX + 2 * side, 7 * NX + 2 * side, 2 + side, 2)

        @pl.when(h == 4)
        def _():
            for side in range(2):
                arrive(g1, g1_recv, 7 + side, 7, 1, (32 * side, 32))
            x_pair(7, 1)
            for side in range(2):
                arrive(g0, g0_recv, 18 + side, 7 * NX + 2 * side, 2)

        @pl.when(h == 1)
        def _():
            for xi in (1, 2):
                arrive(g1, g1_recv, 8 + 8 * xi, xi * NY, 1)
            x_on(2, 0)
            lax.fori_loop(0, rows * per_row, prepare, 0, unroll=4)

        @pl.when((h >= 2) & (h <= 4))
        def _():
            for xi in (1, 2):
                arrive(g1, g1_recv, 8 + 8 * xi + 2 * h - 3, xi * NY + 2 * h - 3, 2)
            x_on(2, 2 * h - 3)
            x_on(1, 2 * h - 2)

        @pl.when(h == 5)
        def _():
            for xi in (1, 2):
                arrive(g1, g1_recv, 8 + 8 * xi + 7, xi * NY + 7, 1)
            x_on(1, 7)
            find_sources()

        @pl.when(h >= 2)
        def _():
            places = (2 * h - 3, (2 * h - 2) * (1 - h // 5))

            def pair(xi, carry):
                @pl.when(xi == 3)
                def _():
                    for yi in places:
                        arrive(g1, g1_recv, 32 + yi, 3 * NY + yi, 1)

                for yi in places:
                    products(xi, yi)
                return carry

            lax.fori_loop(0, NX, pair, 0)

        return carry

    lax.fori_loop(1, 6, gather_step, 0)
    pltpu.make_async_copy(off, off_s, loc_sem.at[8]).wait()

    def landed(m, i):
        total = prod[off_s[m, i]]
        for a in range(1, per_row):
            total = total + prod[off_s[m, a * rows + i]]
        return total

    def piece(n):
        t, j = n // 4 + 1, n % 4
        way, part = j % 2, (j + 1) // 2 % 2
        delta = (5 - j // 2 - t) * (1 - 2 * way)
        return t, way, part, (z + delta + NZ) % NZ

    def core_copy(n):
        return pltpu.make_async_remote_copy(
            src_ref=core_out.at[n], dst_ref=core_in.at[n],
            send_sem=core_send, recv_sem=core_recv.at[n],
            device_id=(me, sibling), device_id_type=MESH,
        )

    def z_copy(n, way):
        return pltpu.make_async_remote_copy(
            src_ref=core_in.at[n], dst_ref=z_in.at[n],
            send_sem=z_send, recv_sem=z_recv.at[n],
            device_id=(me, layer_of(1 - 2 * way)), device_id_type=MESH,
        )

    def give(n):
        _, _, part, to = piece(n)

        def one(i, carry):
            core_out[n, i] = landed(to * 2 + 1 - c, part * 8 + i)
            return carry

        lax.fori_loop(0, 8, one, 0, unroll=4)
        core_copy(n).start()

    def pass_on(n):
        t, way, part, to = piece(n)
        m = to * 2 + c
        core_copy(n).wait_recv()

        @pl.when(t == 1)
        def _():
            def one(i, carry):
                core_in[n, i] = landed(m, part * 8 + i) + core_in[n, i]
                return carry

            lax.fori_loop(0, 8, one, 0, unroll=4)

        @pl.when(t > 1)
        def _():
            z_copy(n - 4, way).wait_recv()

            def one(i, carry):
                core_in[n, i] = landed(m, part * 8 + i) + core_in[n, i] + z_in[n - 4, i]
                return carry

            lax.fori_loop(0, 8, one, 0, unroll=4)

        pl.when(n < 14)(lambda: z_copy(n, way).start())

    lag = 4

    def sum_step(n, carry):
        pl.when(n < 16)(lambda: give(n))
        pl.when(n >= lag)(lambda: pass_on(n - lag))
        return carry

    lax.fori_loop(0, 16 + lag, sum_step, 0)

    loads[4].wait()
    loads[6].wait()
    for part in range(2):
        z_copy(12 + part, 0).wait_recv()

        def one(n, carry):
            i = part * 8 + n
            total = core_in[15 - part, n] + z_in[12 + part, n]
            out_ref[i] = keep_ref[0, i].astype(F32) * (1.5 * cval_ref[i] - 0.5 * total)
            return carry

        lax.fori_loop(0, 8, one, 0, unroll=2)

    for n, buf in enumerate((g0, g1)):
        most = buf.at[pl.ds(0, n_inner - 1)]
        pltpu.make_async_copy(most, most, ag_send.at[n]).wait()
    pltpu.make_async_copy(core_out, core_out, core_send).wait()
    most = core_in.at[pl.ds(0, 14)]
    pltpu.make_async_copy(most, most, z_send).wait()


def body(a_vals, a_cols, b_vals, b_cols, c_cols, c_keep, c_vals):
    n_inner = NX * NY
    a = jnp.transpose(a_vals[0], (1, 0, 2)).reshape(6, 2, 8, 32, 128)
    a = jnp.transpose(a, (0, 1, 3, 2, 4)).reshape(6, 2, 256, 128)
    b = jnp.transpose(b_vals[0].reshape(4, 32, 128), (1, 0, 2)).reshape(128, 128)
    acol = jnp.transpose(a_cols, (2, 0, 1))
    hbm = pl.BlockSpec(memory_space=pltpu.HBM)
    vmem, smem, dma = pltpu.VMEM, pltpu.SMEM, pltpu.SemaphoreType.DMA
    out = pl.pallas_call(
        kernel,
        out_shape=jax.ShapeDtypeStruct((16, 32, 128), F32),
        in_specs=[hbm] * 7,
        out_specs=pl.BlockSpec(memory_space=pltpu.VMEM),
        scratch_shapes=[
            vmem((6, 2, 256, 128), F32),
            vmem((6, 1, 16), I32),
            vmem((128, 128), F32),
            smem((1, 4), I32),
            vmem((16, 16), I32),
            smem((1, 16), I32),
            vmem((16, 32, 128), F32),
            vmem((n_inner, 72, 128), F32),
            vmem((n_inner, 64, 128), F32),
            vmem((96, 64, 128), BF16),
            vmem((n_inner * 4 * CAP + 1, 32, 128), F32),
            vmem((n_inner, 128), I32),
            smem((n_inner, 128), I32),
            vmem((16, 128), I32),
            smem((16, 128), I32),
            vmem((16, 8, 32, 128), F32),
            vmem((16, 8, 32, 128), F32),
            vmem((16, 8, 32, 128), F32),
            dma((9,)),
            dma((2,)),
            dma((20,)),
            dma((40,)),
            dma,
            dma((16,)),
            dma,
            dma((14,)),
        ],
        compiler_params=pltpu.CompilerParams(
            collective_id=0, has_side_effects=True, vmem_limit_bytes=(64 << 20) - (64 << 10)
        ),
        cost_estimate=pl.CostEstimate(flops=1 << 31, bytes_accessed=8 << 20, transcendentals=0),
    )(a, acol, b, b_cols, c_cols, c_keep.T, c_vals.reshape(16, 32, 128))
    return out.reshape(16, 1, 4096)


def solution(mesh):
    in_specs = (
        P("layer", "blk", None, None),
        P("layer", "blk", None),
        P(("blk", "layer"), None, None),
        P(("blk", "layer"), None),
        P("blk", None),
        P("blk", "layer"),
        P("blk", "layer", None),
    )
    out_specs = P("blk", "layer", None)
    return jax.shard_map(body, mesh=mesh, in_specs=in_specs, out_specs=out_specs, check_vma=False)
```

```python
import jax
import jax.numpy as jnp
from jax import lax
from jax.experimental import pallas as pl
from jax.experimental.pallas import tpu as pltpu
from jax.sharding import PartitionSpec as P

NX, NY, NZ = 4, 8, 8
TOP = 48
PARTS = ((0, 1), (1, 2), (3, 1))
CAP = 6
MESH = pl.DeviceIdType.MESH
F32, BF16, I32 = jnp.float32, jnp.bfloat16, jnp.int32
EXACT = lax.Precision.HIGHEST


def kernel(
    a_hbm, acol_hbm, b_hbm, bcol_hbm, ccol_hbm, keep_hbm, cval_hbm, out_ref,
    a_ref, acol_ref, b_ref, bcol_ref, ccol_ref, keep_ref, cval_ref,
    g0, g1, ap, prod, tab, tab_s, off, off_s, core_out, core_in, z_in,
    loc_sem, ag_send, g0_recv, g1_recv, core_send, core_recv, z_send, z_recv,
):
    rows, per_row = 16, 6
    n_inner = NX * NY
    per_k = 4 * CAP
    zero_block = n_inner * per_k
    me, lay = lax.axis_index("blk"), lax.axis_index("layer")
    x, y = me // NY, me % NY
    z, c = lay // 2, lay % 2
    sibling = z * 2 + 1 - c

    def blk_of(dx, dy):
        return (x + dx + NX) % NX * NY + (y + dy + NY) % NY

    def layer_of(dz):
        return (z + dz + NZ) % NZ * 2 + c

    loads = [
        pltpu.make_async_copy(src, dst, loc_sem.at[n])
        for n, (src, dst) in enumerate((
            (b_hbm, b_ref), (bcol_hbm, bcol_ref), (acol_hbm, acol_ref), (ccol_hbm, ccol_ref),
            (keep_hbm, keep_ref), (a_hbm, a_ref), (cval_hbm, cval_ref),
        ))
    ]
    for load in loads:
        load.start()

    steps = ((1, 0), (-1, 0), (0, 1), (0, -1))
    barrier = pltpu.get_barrier_semaphore()
    for step in steps:
        pl.semaphore_signal(barrier, inc=1, device_id=(blk_of(*step), lay), device_id_type=MESH)
    for other in (sibling, layer_of(1), layer_of(-1)):
        pl.semaphore_signal(barrier, inc=1, device_id=(me, other), device_id_type=MESH)

    lane = lax.broadcasted_iota(I32, (32, 128), 1)
    low = lane < 64

    loads[0].wait()
    for pair in range(2):
        first = b_ref[pl.ds(2 * pair, 32, stride=4), :]
        second = b_ref[pl.ds(2 * pair + 1, 32, stride=4), :]
        even = jnp.where(low, first, pltpu.roll(second, 64, 1))
        odd = jnp.where(low, pltpu.roll(first, 64, 1), second)
        for parity, lines in ((0, even), (1, odd)):
            if pair == 0:
                g0[0, pl.ds(parity, TOP // 2, stride=2), :] = lines[:TOP // 2]
                g1[0, pl.ds(64 + parity, 32 - TOP // 2, stride=2), :] = lines[TOP // 2:]
            else:
                g1[0, pl.ds(parity, 32, stride=2), :] = lines
    loads[1].wait()
    sub8 = lax.broadcasted_iota(I32, (8, 128), 0)
    meta = jnp.full((8, 128), -1, I32)
    for s in range(4):
        meta = jnp.where(sub8 == s, bcol_ref[0, s], meta)
    g0[0, TOP:TOP + 8, :] = meta.astype(F32)

    pl.semaphore_wait(barrier, 7)

    def send(buf, recv, n, src, dst, d, count, lines=slice(None)):
        lines = pl.ds(*lines) if isinstance(lines, tuple) else lines
        pltpu.make_async_remote_copy(
            src_ref=buf.at[pl.ds(src, count), lines], dst_ref=buf.at[pl.ds(dst, count), lines],
            send_sem=ag_send.at[0 if buf is g0 else 1], recv_sem=recv.at[n],
            device_id=(blk_of(*steps[d]), lay), device_id_type=MESH,
        ).start()

    def arrive(buf, recv, n, place, count, lines=slice(None)):
        lines = pl.ds(*lines) if isinstance(lines, tuple) else lines
        piece = buf.at[pl.ds(place, count), lines]
        pltpu.make_async_copy(piece, piece, recv.at[n]).wait()

    def row0_on(part):
        src, count = PARTS[part]
        for side in range(2):
            send(g0, g0_recv, 3 * (1 + side) + part, src, (1 + side) * NX + src, 2 + side, count)

    def x_pair(yi, count):
        for d in range(2):
            send(g1, g1_recv, 16 + 8 * (1 - d) + yi, yi, (2 - d) * NY + yi, d, count)

    def x_on(xi, yi):
        send(g1, g1_recv, 32 + yi, xi * NY + yi, 3 * NY + yi, 2 - xi, 1)

    for d in range(2):
        send(g0, g0_recv, 1 - d, 0, 2 - d, d, 1)
    for side in range(2):
        send(g1, g1_recv, 1 + side, 0, 1 + side, 2 + side, 1)
    row0_on(0)
    x_pair(0, 1)

    tile = (lax.broadcasted_iota(I32, (rows, 128), 1) % rows == lax.broadcasted_iota(I32, (rows, 128), 0)).astype(F32)
    loads[2].wait()
    acol = jnp.concatenate([acol_ref[a] for a in range(per_row)], axis=0)
    spread = jnp.dot(acol.astype(F32), tile, preferred_element_type=F32, precision=EXACT)
    lane6 = lax.broadcasted_iota(I32, (per_row, 128), 1)
    mine6 = lane6 // rows == lax.broadcasted_iota(I32, (per_row, 128), 0)
    a_lane = jnp.sum(jnp.where(mine6, spread, 0.0), axis=0, keepdims=True)
    lane1 = lax.broadcasted_iota(I32, (1, 128), 1)
    a_lane = jnp.where(lane1 < rows * per_row, a_lane, -1.0)
    inner = lax.broadcasted_iota(I32, (n_inner, 128), 0).astype(F32)
    onehot = (inner == a_lane).astype(F32)
    before = (lax.broadcasted_iota(I32, (128, 128), 0) < lax.broadcasted_iota(I32, (128, 128), 1)).astype(BF16)
    count = jnp.dot(onehot.astype(BF16), before, preferred_element_type=F32)

    for xi in (1, 2):
        arrive(g0, g0_recv, xi - 1, xi, 1)
    send(g0, g0_recv, 2, 2, 3, 0, 1)
    row0_on(1)

    rank = jnp.sum(onehot * count, axis=0, keepdims=True)
    table = jnp.zeros((n_inner, 128), F32)
    lane_f = lane.astype(F32)
    for r in range(CAP):
        hit = jnp.where(count == float(r), onehot, 0.0)
        table = jnp.where(lane == r, jnp.sum(hit * lane_f, axis=1, keepdims=True), table)
    tab[...] = jnp.clip(table.astype(I32), 0, rows * per_row - 1)
    tab_copy = pltpu.make_async_copy(tab, tab_s, loc_sem.at[7])
    tab_copy.start()
    loads[3].wait()
    target = lax.dot_general(ccol_ref[...].astype(F32), tile, (((0,), (0,)), ((), ())), preferred_element_type=F32, precision=EXACT)
    prod[zero_block] = jnp.zeros((32, 128), F32)
    loads[5].wait()

    arrive(g0, g0_recv, 2, 3, 1)
    row0_on(2)
    tab_copy.wait()

    def prepare(n, carry):
        a, i = n // rows, n % rows
        block = a_ref[a, i // 8, pl.ds(i % 8, 32, stride=8), :]
        high = block.astype(BF16).astype(F32)
        rest = block - high
        ap[n, 0:32, :] = jnp.where(low, high, pltpu.roll(rest, 64, 1)).astype(BF16)
        ap[n, 32:64, :] = jnp.where(low, pltpu.roll(high, 64, 1), rest).astype(BF16)
        return carry

    def inner_at(xi, yi):
        dx = xi + xi // 2 * (5 - 2 * xi)
        dy = (yi + 1) // 2 * (1 - 2 * (yi % 2))
        return (x + dx) % NX * NY + (y + dy + NY) % NY

    def products(xi, yi):
        k = inner_at(xi, yi)
        first = jnp.concatenate([g0[yi * NX + xi, 0:TOP, :], g1[xi * NY + yi, 64:128 - TOP, :]], axis=0)
        right = jnp.concatenate([first, g1[xi * NY + yi, 0:64, :]], axis=1)
        high = right.astype(BF16)
        rest = (right - high.astype(F32)).astype(BF16)
        weights = jnp.concatenate([high, high, rest, rest], axis=0)
        left = jnp.concatenate([ap[tab_s[k, r]] for r in range(CAP)], axis=0)
        left = jnp.concatenate([left, left], axis=1)
        both = jnp.dot(left, weights, preferred_element_type=F32)
        for r in range(CAP):
            for pair in range(2):
                even = both[r * 64:r * 64 + 32, pair * 128:pair * 128 + 128]
                odd = both[r * 64 + 32:r * 64 + 64, pair * 128:pair * 128 + 128]
                prod[k * per_k + 2 * pair * CAP + r] = jnp.where(low, even, pltpu.roll(odd, 64, 1))
                prod[k * per_k + (2 * pair + 1) * CAP + r] = jnp.where(low, pltpu.roll(even, 64, 1), odd)

    def find_sources():
        def pick(k, cols):
            return jnp.where(a_lane == inner_at(k % NX, k // NX).astype(F32), g0[k, TOP:TOP + 8, :], cols)

        cols = lax.fori_loop(0, n_inner, pick, jnp.full((8, 128), -1.0, F32), unroll=8)
        base = a_lane * float(per_k) + rank
        where_from = jnp.full((rows, 128), float(zero_block), F32)
        for s in range(4):
            where_from = jnp.where(target == cols[s:s + 1, :], base + float(CAP * s), where_from)
        off[...] = jnp.clip(where_from.astype(I32), 0, zero_block)
        pltpu.make_async_copy(off, off_s, loc_sem.at[8]).start()

    def gather_step(h, carry):
        early, late = 2 * h - 1, 2 * h
        half = (128 - TOP) // 2

        @pl.when(h <= 3)
        def _():
            for side, yi in ((0, early), (1, late)):
                arrive(g1, g1_recv, yi, yi, 1)

                @pl.when(h <= 2)
                def _():
                    send(g1, g1_recv, yi + 2, yi, yi + 2, 2 + side, 1)

                @pl.when(h == 3)
                def _():
                    send(g1, g1_recv, 7 + side, yi, 7, 2 + side, 1, (half * side, half))

            x_pair(early, 2)
            for part, (src, count) in enumerate(PARTS):
                for side, yi in ((0, early), (1, late)):
                    arrive(g0, g0_recv, 3 * yi + part, yi * NX + src, count)

                    @pl.when(h <= (3 if (part == 1) == (side == 0) else 2))
                    def _():
                        to = yi + 2 - (h // 3 if side == 1 else 0)
                        send(g0, g0_recv, 3 * to + part, yi * NX + src, to * NX + src, 2 + side, count)

        @pl.when(h == 4)
        def _():
            for side in range(2):
                arrive(g1, g1_recv, 7 + side, 7, 1, (half * side, half))
            x_pair(7, 1)
            for part, (src, count) in enumerate(PARTS):
                arrive(g0, g0_recv, 21 + part, 7 * NX + src, count)

        @pl.when(h == 1)
        def _():
            for xi in (1, 2):
                arrive(g1, g1_recv, 8 + 8 * xi, xi * NY, 1)
            x_on(2, 0)
            lax.fori_loop(0, rows * per_row, prepare, 0, unroll=4)

        @pl.when((h >= 2) & (h <= 4))
        def _():
            for xi in (1, 2):
                arrive(g1, g1_recv, 8 + 8 * xi + 2 * h - 3, xi * NY + 2 * h - 3, 2)
            x_on(2, 2 * h - 3)
            x_on(1, 2 * h - 2)

        @pl.when(h == 5)
        def _():
            for xi in (1, 2):
                arrive(g1, g1_recv, 8 + 8 * xi + 7, xi * NY + 7, 1)
            x_on(1, 7)
            find_sources()

        @pl.when(h >= 2)
        def _():
            places = (2 * h - 3, (2 * h - 2) * (1 - h // 5))

            def pair(xi, carry):
                @pl.when(xi == 3)
                def _():
                    for yi in places:
                        arrive(g1, g1_recv, 32 + yi, 3 * NY + yi, 1)

                for yi in places:
                    products(xi, yi)
                return carry

            lax.fori_loop(0, NX, pair, 0)

        return carry

    lax.fori_loop(1, 6, gather_step, 0)
    pltpu.make_async_copy(off, off_s, loc_sem.at[8]).wait()

    def landed(m, i):
        total = prod[off_s[m, i]]
        for a in range(1, per_row):
            total = total + prod[off_s[m, a * rows + i]]
        return total

    def piece(n):
        t, j = n // 4 + 1, n % 4
        way, part = j % 2, (j + 1) // 2 % 2
        delta = (5 - j // 2 - t) * (1 - 2 * way)
        return t, way, part, (z + delta + NZ) % NZ

    def core_copy(n):
        return pltpu.make_async_remote_copy(
            src_ref=core_out.at[n], dst_ref=core_in.at[n],
            send_sem=core_send, recv_sem=core_recv.at[n],
            device_id=(me, sibling), device_id_type=MESH,
        )

    def z_copy(n, way):
        return pltpu.make_async_remote_copy(
            src_ref=core_in.at[n], dst_ref=z_in.at[n],
            send_sem=z_send, recv_sem=z_recv.at[n],
            device_id=(me, layer_of(1 - 2 * way)), device_id_type=MESH,
        )

    def give(n):
        _, _, part, to = piece(n)

        def one(i, carry):
            core_out[n, i] = landed(to * 2 + 1 - c, part * 8 + i)
            return carry

        lax.fori_loop(0, 8, one, 0, unroll=4)
        core_copy(n).start()

    def pass_on(n):
        t, way, part, to = piece(n)
        m = to * 2 + c
        core_copy(n).wait_recv()

        @pl.when(t == 1)
        def _():
            def one(i, carry):
                core_in[n, i] = landed(m, part * 8 + i) + core_in[n, i]
                return carry

            lax.fori_loop(0, 8, one, 0, unroll=4)

        @pl.when(t > 1)
        def _():
            z_copy(n - 4, way).wait_recv()

            def one(i, carry):
                core_in[n, i] = landed(m, part * 8 + i) + core_in[n, i] + z_in[n - 4, i]
                return carry

            lax.fori_loop(0, 8, one, 0, unroll=4)

        pl.when(n < 14)(lambda: z_copy(n, way).start())

    lag = 3

    def sum_step(n, carry):
        pl.when(n < 16)(lambda: give(n))
        pl.when(n >= lag)(lambda: pass_on(n - lag))
        return carry

    lax.fori_loop(0, 16 + lag, sum_step, 0)

    loads[4].wait()
    loads[6].wait()
    for part in range(2):
        z_copy(12 + part, 0).wait_recv()

        def one(n, carry):
            i = part * 8 + n
            total = core_in[15 - part, n] + z_in[12 + part, n]
            out_ref[i] = keep_ref[0, i].astype(F32) * (1.5 * cval_ref[i] - 0.5 * total)
            return carry

        lax.fori_loop(0, 8, one, 0, unroll=2)

    for n, buf in enumerate((g0, g1)):
        most = buf.at[pl.ds(0, n_inner - 1)]
        pltpu.make_async_copy(most, most, ag_send.at[n]).wait()
    pltpu.make_async_copy(core_out, core_out, core_send).wait()
    most = core_in.at[pl.ds(0, 14)]
    pltpu.make_async_copy(most, most, z_send).wait()


def body(a_vals, a_cols, b_vals, b_cols, c_cols, c_keep, c_vals):
    n_inner = NX * NY
    a = jnp.transpose(a_vals[0], (1, 0, 2)).reshape(6, 2, 8, 32, 128)
    a = jnp.transpose(a, (0, 1, 3, 2, 4)).reshape(6, 2, 256, 128)
    b = jnp.transpose(b_vals[0].reshape(4, 32, 128), (1, 0, 2)).reshape(128, 128)
    acol = jnp.transpose(a_cols, (2, 0, 1))
    hbm = pl.BlockSpec(memory_space=pltpu.HBM)
    vmem, smem, dma = pltpu.VMEM, pltpu.SMEM, pltpu.SemaphoreType.DMA
    out = pl.pallas_call(
        kernel,
        out_shape=jax.ShapeDtypeStruct((16, 32, 128), F32),
        in_specs=[hbm] * 7,
        out_specs=pl.BlockSpec(memory_space=pltpu.VMEM),
        scratch_shapes=[
            vmem((6, 2, 256, 128), F32),
            vmem((6, 1, 16), I32),
            vmem((128, 128), F32),
            smem((1, 4), I32),
            vmem((16, 16), I32),
            smem((1, 16), I32),
            vmem((16, 32, 128), F32),
            vmem((n_inner, TOP + 8, 128), F32),
            vmem((n_inner, 128 - TOP, 128), F32),
            vmem((96, 64, 128), BF16),
            vmem((n_inner * 4 * CAP + 1, 32, 128), F32),
            vmem((n_inner, 128), I32),
            smem((n_inner, 128), I32),
            vmem((16, 128), I32),
            smem((16, 128), I32),
            vmem((16, 8, 32, 128), F32),
            vmem((16, 8, 32, 128), F32),
            vmem((16, 8, 32, 128), F32),
            dma((9,)),
            dma((2,)),
            dma((24,)),
            dma((40,)),
            dma,
            dma((16,)),
            dma,
            dma((14,)),
        ],
        compiler_params=pltpu.CompilerParams(
            collective_id=0, has_side_effects=True, vmem_limit_bytes=(64 << 20) - (64 << 10)
        ),
        cost_estimate=pl.CostEstimate(flops=1 << 31, bytes_accessed=8 << 20, transcendentals=0),
    )(a, acol, b, b_cols, c_cols, c_keep.T, c_vals.reshape(16, 32, 128))
    return out.reshape(16, 1, 4096)


def solution(mesh):
    in_specs = (
        P("layer", "blk", None, None),
        P("layer", "blk", None),
        P(("blk", "layer"), None, None),
        P(("blk", "layer"), None),
        P("blk", None),
        P("blk", "layer"),
        P("blk", "layer", None),
    )
    out_specs = P("blk", "layer", None)
    return jax.shard_map(body, mesh=mesh, in_specs=in_specs, out_specs=out_specs, check_vma=False)
```

```python
import jax
import jax.numpy as jnp
from jax import lax
from jax.experimental import pallas as pl
from jax.experimental.pallas import tpu as pltpu
from jax.sharding import PartitionSpec as P

NX, NY, NZ = 4, 8, 8
TOP = 48
PARTS = ((0, 1), (1, 2), (3, 1))
CAP = 6
MESH = pl.DeviceIdType.MESH
F32, BF16, I32 = jnp.float32, jnp.bfloat16, jnp.int32
EXACT = lax.Precision.HIGHEST


def kernel(
    a_hbm, acol_hbm, b_hbm, bcol_hbm, ccol_hbm, keep_hbm, cval_hbm, out_ref,
    a_ref, acol_ref, b_ref, bcol_ref, ccol_ref, keep_ref, cval_ref,
    g0, g1, ap, prod, tab, tab_s, off, off_s, core_out, core_in, z_in,
    loc_sem, ag_send, g0_recv, g1_recv, core_send, core_recv, z_send, z_recv,
):
    rows, per_row = 16, 6
    n_inner = NX * NY
    per_k = 4 * CAP
    zero_block = n_inner * per_k
    me, lay = lax.axis_index("blk"), lax.axis_index("layer")
    x, y = me // NY, me % NY
    z, c = lay // 2, lay % 2
    sibling = z * 2 + 1 - c

    def blk_of(dx, dy):
        return (x + dx + NX) % NX * NY + (y + dy + NY) % NY

    def layer_of(dz):
        return (z + dz + NZ) % NZ * 2 + c

    loads = [
        pltpu.make_async_copy(src, dst, loc_sem.at[n])
        for n, (src, dst) in enumerate((
            (b_hbm, b_ref), (bcol_hbm, bcol_ref), (acol_hbm, acol_ref), (ccol_hbm, ccol_ref),
            (keep_hbm, keep_ref), (a_hbm, a_ref), (cval_hbm, cval_ref),
        ))
    ]
    for load in loads:
        load.start()

    steps = ((1, 0), (-1, 0), (0, 1), (0, -1))
    barrier = pltpu.get_barrier_semaphore()
    for step in steps:
        pl.semaphore_signal(barrier, inc=1, device_id=(blk_of(*step), lay), device_id_type=MESH)
    for other in (sibling, layer_of(1), layer_of(-1)):
        pl.semaphore_signal(barrier, inc=1, device_id=(me, other), device_id_type=MESH)

    lane = lax.broadcasted_iota(I32, (32, 128), 1)
    low = lane < 64

    loads[0].wait()
    for pair in range(2):
        first = b_ref[pl.ds(2 * pair, 32, stride=4), :]
        second = b_ref[pl.ds(2 * pair + 1, 32, stride=4), :]
        even = jnp.where(low, first, pltpu.roll(second, 64, 1))
        odd = jnp.where(low, pltpu.roll(first, 64, 1), second)
        for parity, lines in ((0, even), (1, odd)):
            if pair == 0:
                g0[0, pl.ds(parity, TOP // 2, stride=2), :] = lines[:TOP // 2]
                g1[0, pl.ds(64 + parity, 32 - TOP // 2, stride=2), :] = lines[TOP // 2:]
            else:
                g1[0, pl.ds(parity, 32, stride=2), :] = lines
    loads[1].wait()
    sub8 = lax.broadcasted_iota(I32, (8, 128), 0)
    meta = jnp.full((8, 128), -1, I32)
    for s in range(4):
        meta = jnp.where(sub8 == s, bcol_ref[0, s], meta)
    g0[0, TOP:TOP + 8, :] = meta.astype(F32)

    pl.semaphore_wait(barrier, 7)

    def send(buf, recv, n, src, dst, d, count, lines=slice(None)):
        lines = pl.ds(*lines) if isinstance(lines, tuple) else lines
        pltpu.make_async_remote_copy(
            src_ref=buf.at[pl.ds(src, count), lines], dst_ref=buf.at[pl.ds(dst, count), lines],
            send_sem=ag_send.at[0 if buf is g0 else 1], recv_sem=recv.at[n],
            device_id=(blk_of(*steps[d]), lay), device_id_type=MESH,
        ).start()

    def arrive(buf, recv, n, place, count, lines=slice(None)):
        lines = pl.ds(*lines) if isinstance(lines, tuple) else lines
        piece = buf.at[pl.ds(place, count), lines]
        pltpu.make_async_copy(piece, piece, recv.at[n]).wait()

    def row0_on(part):
        src, count = PARTS[part]
        for side in range(2):
            send(g0, g0_recv, 3 * (1 + side) + part, src, (1 + side) * NX + src, 2 + side, count)

    def x_pair(yi, count):
        for d in range(2):
            send(g1, g1_recv, 16 + 8 * (1 - d) + yi, yi, (2 - d) * NY + yi, d, count)

    def x_on(xi, yi):
        send(g1, g1_recv, 32 + yi, xi * NY + yi, 3 * NY + yi, 2 - xi, 1)

    for d in range(2):
        send(g0, g0_recv, 1 - d, 0, 2 - d, d, 1)
    for side in range(2):
        send(g1, g1_recv, 1 + side, 0, 1 + side, 2 + side, 1)
    row0_on(0)
    x_pair(0, 1)

    tile = (lax.broadcasted_iota(I32, (rows, 128), 1) % rows == lax.broadcasted_iota(I32, (rows, 128), 0)).astype(F32)
    loads[2].wait()
    acol = jnp.concatenate([acol_ref[a] for a in range(per_row)], axis=0)
    spread = jnp.dot(acol.astype(F32), tile, preferred_element_type=F32, precision=EXACT)
    lane6 = lax.broadcasted_iota(I32, (per_row, 128), 1)
    mine6 = lane6 // rows == lax.broadcasted_iota(I32, (per_row, 128), 0)
    a_lane = jnp.sum(jnp.where(mine6, spread, 0.0), axis=0, keepdims=True)
    lane1 = lax.broadcasted_iota(I32, (1, 128), 1)
    a_lane = jnp.where(lane1 < rows * per_row, a_lane, -1.0)
    inner = lax.broadcasted_iota(I32, (n_inner, 128), 0).astype(F32)
    onehot = (inner == a_lane).astype(F32)
    before = (lax.broadcasted_iota(I32, (128, 128), 0) < lax.broadcasted_iota(I32, (128, 128), 1)).astype(BF16)
    count = jnp.dot(onehot.astype(BF16), before, preferred_element_type=F32)

    for xi in (1, 2):
        arrive(g0, g0_recv, xi - 1, xi, 1)
    send(g0, g0_recv, 2, 2, 3, 0, 1)
    row0_on(1)

    rank = jnp.sum(onehot * count, axis=0, keepdims=True)
    table = jnp.zeros((n_inner, 128), F32)
    lane_f = lane.astype(F32)
    for r in range(CAP):
        hit = jnp.where(count == float(r), onehot, 0.0)
        table = jnp.where(lane == r, jnp.sum(hit * lane_f, axis=1, keepdims=True), table)
    tab[...] = jnp.clip(table.astype(I32), 0, rows * per_row - 1)
    tab_copy = pltpu.make_async_copy(tab, tab_s, loc_sem.at[7])
    tab_copy.start()
    loads[3].wait()
    target = lax.dot_general(ccol_ref[...].astype(F32), tile, (((0,), (0,)), ((), ())), preferred_element_type=F32, precision=EXACT)
    prod[zero_block] = jnp.zeros((32, 128), F32)
    loads[5].wait()

    arrive(g0, g0_recv, 2, 3, 1)
    row0_on(2)
    tab_copy.wait()

    def prepare(group, carry):
        blocks = []
        for n in range(4):
            a, i = group // 4, group % 4 * 4 + n
            blocks.append(a_ref[a, i // 8, pl.ds(i % 8, 32, stride=8), :])
        for n, block in enumerate(blocks):
            high = block.astype(BF16).astype(F32)
            rest = block - high
            ap[group * 4 + n, 0:32, :] = jnp.where(low, high, pltpu.roll(rest, 64, 1)).astype(BF16)
            ap[group * 4 + n, 32:64, :] = jnp.where(low, pltpu.roll(high, 64, 1), rest).astype(BF16)
        return carry

    def inner_at(xi, yi):
        dx = xi + xi // 2 * (5 - 2 * xi)
        dy = (yi + 1) // 2 * (1 - 2 * (yi % 2))
        return (x + dx) % NX * NY + (y + dy + NY) % NY

    def factors(xi, yi):
        k = inner_at(xi, yi)
        first = jnp.concatenate([g0[yi * NX + xi, 0:TOP, :], g1[xi * NY + yi, 64:128 - TOP, :]], axis=0)
        right = jnp.concatenate([first, g1[xi * NY + yi, 0:64, :]], axis=1)
        high = right.astype(BF16)
        rest = (right - high.astype(F32)).astype(BF16)
        weights = jnp.concatenate([high, high, rest, rest], axis=0)
        left = jnp.concatenate([ap[tab_s[k, r]] for r in range(CAP)], axis=0)
        return k, jnp.concatenate([left, left], axis=1), weights

    def keep_products(k, both):
        for r in range(CAP):
            for pair in range(2):
                even = both[r * 64:r * 64 + 32, pair * 128:pair * 128 + 128]
                odd = both[r * 64 + 32:r * 64 + 64, pair * 128:pair * 128 + 128]
                prod[k * per_k + 2 * pair * CAP + r] = jnp.where(low, even, pltpu.roll(odd, 64, 1))
                prod[k * per_k + (2 * pair + 1) * CAP + r] = jnp.where(low, pltpu.roll(even, 64, 1), odd)

    def products(xi, places):
        both = [factors(xi, yi) for yi in places]
        both = [(k, jnp.dot(left, weights, preferred_element_type=F32)) for k, left, weights in both]
        for k, values in both:
            keep_products(k, values)

    def find_sources():
        def pick(k, cols):
            return jnp.where(a_lane == inner_at(k % NX, k // NX).astype(F32), g0[k, TOP:TOP + 8, :], cols)

        cols = lax.fori_loop(0, n_inner, pick, jnp.full((8, 128), -1.0, F32), unroll=8)
        base = a_lane * float(per_k) + rank
        where_from = jnp.full((rows, 128), float(zero_block), F32)
        for s in range(4):
            where_from = jnp.where(target == cols[s:s + 1, :], base + float(CAP * s), where_from)
        off[...] = jnp.clip(where_from.astype(I32), 0, zero_block)
        pltpu.make_async_copy(off, off_s, loc_sem.at[8]).start()

    def gather_step(h, carry):
        early, late = 2 * h - 1, 2 * h
        half = (128 - TOP) // 2

        @pl.when(h <= 3)
        def _():
            for side, yi in ((0, early), (1, late)):
                arrive(g1, g1_recv, yi, yi, 1)

                @pl.when(h <= 2)
                def _():
                    send(g1, g1_recv, yi + 2, yi, yi + 2, 2 + side, 1)

                @pl.when(h == 3)
                def _():
                    send(g1, g1_recv, 7 + side, yi, 7, 2 + side, 1, (half * side, half))

            x_pair(early, 2)
            for part, (src, count) in enumerate(PARTS):
                for side, yi in ((0, early), (1, late)):
                    arrive(g0, g0_recv, 3 * yi + part, yi * NX + src, count)

                    @pl.when(h <= (3 if (part == 1) == (side == 0) else 2))
                    def _():
                        to = yi + 2 - (h // 3 if side == 1 else 0)
                        send(g0, g0_recv, 3 * to + part, yi * NX + src, to * NX + src, 2 + side, count)

        @pl.when(h == 4)
        def _():
            for side in range(2):
                arrive(g1, g1_recv, 7 + side, 7, 1, (half * side, half))
            x_pair(7, 1)
            for part, (src, count) in enumerate(PARTS):
                arrive(g0, g0_recv, 21 + part, 7 * NX + src, count)

        @pl.when(h == 1)
        def _():
            for xi in (1, 2):
                arrive(g1, g1_recv, 8 + 8 * xi, xi * NY, 1)
            x_on(2, 0)
            lax.fori_loop(0, rows * per_row // 4, prepare, 0, unroll=2)

        @pl.when((h >= 2) & (h <= 4))
        def _():
            for xi in (1, 2):
                arrive(g1, g1_recv, 8 + 8 * xi + 2 * h - 3, xi * NY + 2 * h - 3, 2)
            x_on(2, 2 * h - 3)
            x_on(1, 2 * h - 2)

        @pl.when(h == 5)
        def _():
            for xi in (1, 2):
                arrive(g1, g1_recv, 8 + 8 * xi + 7, xi * NY + 7, 1)
            x_on(1, 7)
            find_sources()

        @pl.when(h >= 2)
        def _():
            places = (2 * h - 3, (2 * h - 2) * (1 - h // 5))

            def pair(xi, carry):
                @pl.when(xi == 3)
                def _():
                    for yi in places:
                        arrive(g1, g1_recv, 32 + yi, 3 * NY + yi, 1)

                products(xi, places)
                return carry

            lax.fori_loop(0, NX, pair, 0)

        return carry

    lax.fori_loop(1, 6, gather_step, 0)
    pltpu.make_async_copy(off, off_s, loc_sem.at[8]).wait()

    def landed(m, i):
        total = prod[off_s[m, i]]
        for a in range(1, per_row):
            total = total + prod[off_s[m, a * rows + i]]
        return total

    def piece(n):
        t, j = n // 8 + 1, n % 8
        way = j % 2
        row = (way + j // 4) % 2 * 8 + j // 2 % 2 * 4
        delta = (5 - j // 4 - t) * (1 - 2 * way)
        return t, way, row, (z + delta + NZ) % NZ

    def core_copy(n):
        return pltpu.make_async_remote_copy(
            src_ref=core_out.at[n], dst_ref=core_in.at[n],
            send_sem=core_send, recv_sem=core_recv.at[n],
            device_id=(me, sibling), device_id_type=MESH,
        )

    def z_copy(n, way):
        return pltpu.make_async_remote_copy(
            src_ref=core_in.at[n], dst_ref=z_in.at[n],
            send_sem=z_send, recv_sem=z_recv.at[n],
            device_id=(me, layer_of(1 - 2 * way)), device_id_type=MESH,
        )

    def give(n):
        _, _, row, to = piece(n)
        sums = [landed(to * 2 + 1 - c, row + i) for i in range(4)]
        for i in range(4):
            core_out[n, i] = sums[i]
        core_copy(n).start()

    def pass_on(n):
        t, way, row, to = piece(n)
        core_copy(n).wait_recv()

        @pl.when(t == 1)
        def _():
            sums = [landed(to * 2 + c, row + i) + core_in[n, i] for i in range(4)]
            for i in range(4):
                core_in[n, i] = sums[i]

        @pl.when(t > 1)
        def _():
            z_copy(n - 8, way).wait_recv()
            sums = [landed(to * 2 + c, row + i) + core_in[n, i] + z_in[n - 8, i] for i in range(4)]
            for i in range(4):
                core_in[n, i] = sums[i]

        pl.when(n < 28)(lambda: z_copy(n, way).start())

    lag = 6

    def sum_step(n, carry):
        pl.when(n < 32)(lambda: give(n))
        pl.when(n >= lag)(lambda: pass_on(n - lag))
        return carry

    lax.fori_loop(0, 32 + lag, sum_step, 0)

    loads[4].wait()
    loads[6].wait()
    for n in range(24, 28):
        mine = n + 5 - n % 2 * 2
        row = (1 - n % 2 + 1) % 2 * 8 + n // 2 % 2 * 4
        z_copy(n, 0).wait_recv()
        for i in range(4):
            total = core_in[mine, i] + z_in[n, i]
            out_ref[row + i] = keep_ref[0, row + i].astype(F32) * (1.5 * cval_ref[row + i] - 0.5 * total)

    for n, buf in enumerate((g0, g1)):
        most = buf.at[pl.ds(0, n_inner - 1)]
        pltpu.make_async_copy(most, most, ag_send.at[n]).wait()
    pltpu.make_async_copy(core_out, core_out, core_send).wait()
    most = core_in.at[pl.ds(0, 28)]
    pltpu.make_async_copy(most, most, z_send).wait()


def body(a_vals, a_cols, b_vals, b_cols, c_cols, c_keep, c_vals):
    n_inner = NX * NY
    a = jnp.transpose(a_vals[0], (1, 0, 2)).reshape(6, 2, 8, 32, 128)
    a = jnp.transpose(a, (0, 1, 3, 2, 4)).reshape(6, 2, 256, 128)
    b = jnp.transpose(b_vals[0].reshape(4, 32, 128), (1, 0, 2)).reshape(128, 128)
    acol = jnp.transpose(a_cols, (2, 0, 1))
    hbm = pl.BlockSpec(memory_space=pltpu.HBM)
    vmem, smem, dma = pltpu.VMEM, pltpu.SMEM, pltpu.SemaphoreType.DMA
    out = pl.pallas_call(
        kernel,
        out_shape=jax.ShapeDtypeStruct((16, 32, 128), F32),
        in_specs=[hbm] * 7,
        out_specs=pl.BlockSpec(memory_space=pltpu.VMEM),
        scratch_shapes=[
            vmem((6, 2, 256, 128), F32),
            vmem((6, 1, 16), I32),
            vmem((128, 128), F32),
            smem((1, 4), I32),
            vmem((16, 16), I32),
            smem((1, 16), I32),
            vmem((16, 32, 128), F32),
            vmem((n_inner, TOP + 8, 128), F32),
            vmem((n_inner, 128 - TOP, 128), F32),
            vmem((96, 64, 128), BF16),
            vmem((n_inner * 4 * CAP + 1, 32, 128), F32),
            vmem((n_inner, 128), I32),
            smem((n_inner, 128), I32),
            vmem((16, 128), I32),
            smem((16, 128), I32),
            vmem((32, 4, 32, 128), F32),
            vmem((32, 4, 32, 128), F32),
            vmem((32, 4, 32, 128), F32),
            dma((9,)),
            dma((2,)),
            dma((24,)),
            dma((40,)),
            dma,
            dma((32,)),
            dma,
            dma((28,)),
        ],
        compiler_params=pltpu.CompilerParams(
            collective_id=0, has_side_effects=True, vmem_limit_bytes=(64 << 20) - (64 << 10)
        ),
        cost_estimate=pl.CostEstimate(flops=1 << 31, bytes_accessed=8 << 20, transcendentals=0),
    )(a, acol, b, b_cols, c_cols, c_keep.T, c_vals.reshape(16, 32, 128))
    return out.reshape(16, 1, 4096)


def solution(mesh):
    in_specs = (
        P("layer", "blk", None, None),
        P("layer", "blk", None),
        P(("blk", "layer"), None, None),
        P(("blk", "layer"), None),
        P("blk", None),
        P("blk", "layer"),
        P("blk", "layer", None),
    )
    out_specs = P("blk", "layer", None)
    return jax.shard_map(body, mesh=mesh, in_specs=in_specs, out_specs=out_specs, check_vma=False)
```

```python
import jax
import jax.numpy as jnp
from jax import lax
from jax.experimental import pallas as pl
from jax.experimental.pallas import tpu as pltpu
from jax.sharding import PartitionSpec as P

NX, NY, NZ = 4, 8, 8
TOP = 48
PARTS = ((0, 1), (1, 2), (3, 1))
CAP = 6
MESH = pl.DeviceIdType.MESH
F32, BF16, I32 = jnp.float32, jnp.bfloat16, jnp.int32


def kernel(
    a_hbm, acol_hbm, b_hbm, bcol_hbm, ccol_hbm, keep_hbm, cval_hbm, out_ref,
    a_ref, acol_ref, b_ref, bcol_ref, ccol_ref, keep_ref, cval_ref,
    g0, g1, ap, prod, tab, tab_s, off, off_s, core_out, core_in, z_in,
    loc_sem, ag_send, g0_recv, g1_recv, core_send, core_recv, z_send, z_recv,
):
    rows, per_row = 16, 6
    n_inner = NX * NY
    per_k = 4 * CAP
    zero_block = n_inner * per_k
    me, lay = lax.axis_index("blk"), lax.axis_index("layer")
    x, y = me // NY, me % NY
    z, c = lay // 2, lay % 2
    sibling = z * 2 + 1 - c

    def blk_of(dx, dy):
        return (x + dx + NX) % NX * NY + (y + dy + NY) % NY

    def layer_of(dz):
        return (z + dz + NZ) % NZ * 2 + c

    steps = ((1, 0), (-1, 0), (0, 1), (0, -1))
    barrier = pltpu.get_barrier_semaphore()
    for step in steps:
        pl.semaphore_signal(barrier, inc=1, device_id=(blk_of(*step), lay), device_id_type=MESH)
    for other in (sibling, layer_of(1), layer_of(-1)):
        pl.semaphore_signal(barrier, inc=1, device_id=(me, other), device_id_type=MESH)

    loads = [
        pltpu.make_async_copy(src, dst, loc_sem.at[n])
        for n, (src, dst) in enumerate((
            (b_hbm, b_ref), (bcol_hbm, bcol_ref), (acol_hbm, acol_ref), (ccol_hbm, ccol_ref),
            (keep_hbm, keep_ref), (a_hbm, a_ref), (cval_hbm, cval_ref),
        ))
    ]
    for load in loads:
        load.start()

    lane = lax.broadcasted_iota(I32, (32, 128), 1)
    low = lane < 64

    loads[0].wait()
    for pair in range(2):
        first = b_ref[pl.ds(2 * pair, 32, stride=4), :]
        second = b_ref[pl.ds(2 * pair + 1, 32, stride=4), :]
        even = jnp.where(low, first, pltpu.roll(second, 64, 1))
        odd = jnp.where(low, pltpu.roll(first, 64, 1), second)
        for parity, lines in ((0, even), (1, odd)):
            if pair == 0:
                g0[0, pl.ds(parity, TOP // 2, stride=2), :] = lines[:TOP // 2]
                g1[0, pl.ds(64 + parity, 32 - TOP // 2, stride=2), :] = lines[TOP // 2:]
            else:
                g1[0, pl.ds(parity, 32, stride=2), :] = lines
    loads[1].wait()
    sub8 = lax.broadcasted_iota(I32, (8, 128), 0)
    meta = jnp.full((8, 128), -1, I32)
    for s in range(4):
        meta = jnp.where(sub8 == s, bcol_ref[0, s], meta)
    g0[0, TOP:TOP + 8, :] = meta.astype(F32)

    pl.semaphore_wait(barrier, 7)

    def send(buf, recv, n, src, dst, d, count, lines=slice(None)):
        lines = pl.ds(*lines) if isinstance(lines, tuple) else lines
        pltpu.make_async_remote_copy(
            src_ref=buf.at[pl.ds(src, count), lines], dst_ref=buf.at[pl.ds(dst, count), lines],
            send_sem=ag_send.at[0 if buf is g0 else 1], recv_sem=recv.at[n],
            device_id=(blk_of(*steps[d]), lay), device_id_type=MESH,
        ).start()

    def arrive(buf, recv, n, place, count, lines=slice(None)):
        lines = pl.ds(*lines) if isinstance(lines, tuple) else lines
        piece = buf.at[pl.ds(place, count), lines]
        pltpu.make_async_copy(piece, piece, recv.at[n]).wait()

    def row0_on(part):
        src, count = PARTS[part]
        for side in range(2):
            send(g0, g0_recv, 3 * (1 + side) + part, src, (1 + side) * NX + src, 2 + side, count)

    def x_pair(yi, count):
        for d in range(2):
            send(g1, g1_recv, 16 + 8 * (1 - d) + yi, yi, (2 - d) * NY + yi, d, count)

    def x_on(xi, yi):
        send(g1, g1_recv, 32 + yi, xi * NY + yi, 3 * NY + yi, 2 - xi, 1)

    for d in range(2):
        send(g0, g0_recv, 1 - d, 0, 2 - d, d, 1)
    for side in range(2):
        send(g1, g1_recv, 1 + side, 0, 1 + side, 2 + side, 1)
    row0_on(0)
    x_pair(0, 1)

    tile = (lax.broadcasted_iota(I32, (rows, 128), 1) % rows == lax.broadcasted_iota(I32, (rows, 128), 0)).astype(BF16)
    loads[2].wait()
    acol = jnp.concatenate([acol_ref[a] for a in range(per_row)], axis=0)
    spread = jnp.dot(acol.astype(F32).astype(BF16), tile, preferred_element_type=F32)
    lane6 = lax.broadcasted_iota(I32, (per_row, 128), 1)
    mine6 = lane6 // rows == lax.broadcasted_iota(I32, (per_row, 128), 0)
    a_lane = jnp.sum(jnp.where(mine6, spread, 0.0), axis=0, keepdims=True)
    lane1 = lax.broadcasted_iota(I32, (1, 128), 1)
    a_lane = jnp.where(lane1 < rows * per_row, a_lane, -1.0)
    inner = lax.broadcasted_iota(I32, (n_inner, 128), 0).astype(F32)
    onehot = (inner == a_lane).astype(F32)
    before = (lax.broadcasted_iota(I32, (128, 128), 0) < lax.broadcasted_iota(I32, (128, 128), 1)).astype(BF16)
    count = jnp.dot(onehot.astype(BF16), before, preferred_element_type=F32)

    for xi in (1, 2):
        arrive(g0, g0_recv, xi - 1, xi, 1)
    send(g0, g0_recv, 2, 2, 3, 0, 1)
    row0_on(1)

    rank = jnp.sum(onehot * count, axis=0, keepdims=True)
    table = jnp.zeros((n_inner, 128), F32)
    lane_f = lane.astype(F32)
    for r in range(CAP):
        hit = jnp.where(count == float(r), onehot, 0.0)
        table = jnp.where(lane == r, jnp.sum(hit * lane_f, axis=1, keepdims=True), table)
    tab[...] = jnp.clip(table.astype(I32), 0, rows * per_row - 1)
    tab_copy = pltpu.make_async_copy(tab, tab_s, loc_sem.at[7])
    tab_copy.start()
    loads[3].wait()
    ccol = ccol_ref[...]
    digits = jnp.concatenate([ccol // 16, ccol % 16], axis=1).astype(F32).astype(BF16)
    digits = lax.dot_general(digits, tile, (((0,), (0,)), ((), ())), preferred_element_type=F32)
    target = digits[:rows] * 16.0 + digits[rows:]
    prod[zero_block] = jnp.zeros((32, 128), F32)
    loads[5].wait()

    arrive(g0, g0_recv, 2, 3, 1)
    row0_on(2)

    def prepare(group, carry):
        blocks = []
        for n in range(4):
            a, i = group // 4, group % 4 * 4 + n
            blocks.append(a_ref[a, i // 8, pl.ds(i % 8, 32, stride=8), :])
        for n, block in enumerate(blocks):
            turned = pltpu.roll(block, 64, 1)
            for parity, twice in enumerate((jnp.where(low, block, turned), jnp.where(low, turned, block))):
                high = twice.astype(BF16).astype(F32)
                ap[group * 4 + n, 32 * parity:32 * parity + 32, :] = jnp.where(low, high, twice - high).astype(BF16)
        return carry

    def inner_at(xi, yi):
        dx = xi + xi // 2 * (5 - 2 * xi)
        dy = (yi + 1) // 2 * (1 - 2 * (yi % 2))
        return (x + dx) % NX * NY + (y + dy + NY) % NY

    def factors(xi, yi):
        k = inner_at(xi, yi)
        first = jnp.concatenate([g0[yi * NX + xi, 0:TOP, :], g1[xi * NY + yi, 64:128 - TOP, :]], axis=0)
        right = jnp.concatenate([first, g1[xi * NY + yi, 0:64, :]], axis=1)
        high = right.astype(BF16)
        rest = (right - high.astype(F32)).astype(BF16)
        weights = jnp.concatenate([high, high, rest, rest], axis=0)
        left = jnp.concatenate([ap[tab_s[k, r]] for r in range(CAP)], axis=0)
        return k, jnp.concatenate([left, left], axis=1), weights

    def keep_products(k, both):
        for r in range(CAP):
            for pair in range(2):
                even = both[r * 64:r * 64 + 32, pair * 128:pair * 128 + 128]
                odd = both[r * 64 + 32:r * 64 + 64, pair * 128:pair * 128 + 128]
                moved = pltpu.roll(jnp.where(low, odd, even), 64, 1)
                prod[k * per_k + 2 * pair * CAP + r] = jnp.where(low, even, moved)
                prod[k * per_k + (2 * pair + 1) * CAP + r] = jnp.where(low, moved, odd)

    def products(xi, places):
        both = [factors(xi, yi) for yi in places]
        both = [(k, jnp.dot(left, weights, preferred_element_type=F32)) for k, left, weights in both]
        for k, values in both:
            keep_products(k, values)

    def find_sources():
        def pick(k, cols):
            return jnp.where(a_lane == inner_at(k % NX, k // NX).astype(F32), g0[k, TOP:TOP + 8, :], cols)

        cols = lax.fori_loop(0, n_inner, pick, jnp.full((8, 128), -1.0, F32), unroll=8)
        base = a_lane * float(per_k) + rank
        where_from = jnp.full((rows, 128), float(zero_block), F32)
        for s in range(4):
            where_from = jnp.where(target == cols[s:s + 1, :], base + float(CAP * s), where_from)
        off[...] = jnp.clip(where_from.astype(I32), 0, zero_block)
        pltpu.make_async_copy(off, off_s, loc_sem.at[8]).start()

    def gather_step(h, carry):
        early, late = 2 * h - 1, 2 * h
        half = (128 - TOP) // 2

        @pl.when(h <= 3)
        def _():
            for side, yi in ((0, early), (1, late)):
                arrive(g1, g1_recv, yi, yi, 1)

                @pl.when(h <= 2)
                def _():
                    send(g1, g1_recv, yi + 2, yi, yi + 2, 2 + side, 1)

                @pl.when(h == 3)
                def _():
                    send(g1, g1_recv, 7 + side, yi, 7, 2 + side, 1, (half * side, half))

            x_pair(early, 2)
            for part, (src, count) in enumerate(PARTS):
                for side, yi in ((0, early), (1, late)):
                    arrive(g0, g0_recv, 3 * yi + part, yi * NX + src, count)

                    @pl.when(h <= (3 if (part == 1) == (side == 0) else 2))
                    def _():
                        to = yi + 2 - (h // 3 if side == 1 else 0)
                        send(g0, g0_recv, 3 * to + part, yi * NX + src, to * NX + src, 2 + side, count)

        @pl.when(h == 4)
        def _():
            for side in range(2):
                arrive(g1, g1_recv, 7 + side, 7, 1, (half * side, half))
            x_pair(7, 1)
            for part, (src, count) in enumerate(PARTS):
                arrive(g0, g0_recv, 21 + part, 7 * NX + src, count)

        @pl.when(h == 1)
        def _():
            for xi in (1, 2):
                arrive(g1, g1_recv, 8 + 8 * xi, xi * NY, 1)
            x_on(2, 0)
            lax.fori_loop(0, rows * per_row // 4, prepare, 0, unroll=2)

        @pl.when((h >= 2) & (h <= 4))
        def _():
            for xi in (1, 2):
                arrive(g1, g1_recv, 8 + 8 * xi + 2 * h - 3, xi * NY + 2 * h - 3, 2)
            x_on(2, 2 * h - 3)
            x_on(1, 2 * h - 2)

        @pl.when(h == 5)
        def _():
            for xi in (1, 2):
                arrive(g1, g1_recv, 8 + 8 * xi + 7, xi * NY + 7, 1)
            x_on(1, 7)
            find_sources()

        @pl.when(h >= 2)
        def _():
            pl.when(h == 2)(tab_copy.wait)
            places = (2 * h - 3, (2 * h - 2) * (1 - h // 5))

            def pair(xi, carry):
                @pl.when(xi == 3)
                def _():
                    for yi in places:
                        arrive(g1, g1_recv, 32 + yi, 3 * NY + yi, 1)

                products(xi, places)
                return carry

            lax.fori_loop(0, NX, pair, 0)

        return carry

    lax.fori_loop(1, 6, gather_step, 0)
    pltpu.make_async_copy(off, off_s, loc_sem.at[8]).wait()

    def landed(m, i):
        total = prod[off_s[m, i]]
        for a in range(1, per_row):
            total = total + prod[off_s[m, a * rows + i]]
        return total

    def piece(n):
        t, j = n // 8 + 1, n % 8
        way = j % 2
        row = (way + j // 4) % 2 * 8 + j // 2 % 2 * 4
        delta = (5 - j // 4 - t) * (1 - 2 * way)
        return t, way, row, (z + delta + NZ) % NZ

    def core_copy(n):
        return pltpu.make_async_remote_copy(
            src_ref=core_out.at[n], dst_ref=core_in.at[n],
            send_sem=core_send, recv_sem=core_recv.at[n],
            device_id=(me, sibling), device_id_type=MESH,
        )

    def z_copy(n, way):
        return pltpu.make_async_remote_copy(
            src_ref=core_in.at[n], dst_ref=z_in.at[n],
            send_sem=z_send, recv_sem=z_recv.at[n],
            device_id=(me, layer_of(1 - 2 * way)), device_id_type=MESH,
        )

    def give(n):
        _, _, row, to = piece(n)
        sums = [landed(to * 2 + 1 - c, row + i) for i in range(4)]
        for i in range(4):
            core_out[n, i] = sums[i]
        core_copy(n).start()

    def pass_on(n):
        t, way, row, to = piece(n)
        core_copy(n).wait_recv()

        @pl.when(t == 1)
        def _():
            sums = [landed(to * 2 + c, row + i) + core_in[n, i] for i in range(4)]
            for i in range(4):
                core_in[n, i] = sums[i]

        @pl.when(t > 1)
        def _():
            z_copy(n - 8, way).wait_recv()
            sums = [landed(to * 2 + c, row + i) + core_in[n, i] + z_in[n - 8, i] for i in range(4)]
            for i in range(4):
                core_in[n, i] = sums[i]

        pl.when(n < 28)(lambda: z_copy(n, way).start())

    lag = 6

    def sum_step(n, carry):
        pl.when(n < 32)(lambda: give(n))
        pl.when(n >= lag)(lambda: pass_on(n - lag))
        return carry

    lax.fori_loop(0, 32 + lag, sum_step, 0)

    loads[4].wait()
    loads[6].wait()
    for n in range(24, 28):
        mine = n + 5 - n % 2 * 2
        row = (1 - n % 2 + 1) % 2 * 8 + n // 2 % 2 * 4
        z_copy(n, 0).wait_recv()
        for i in range(4):
            total = core_in[mine, i] + z_in[n, i]
            out_ref[row + i] = keep_ref[0, row + i].astype(F32) * (1.5 * cval_ref[row + i] - 0.5 * total)

    for n, buf in enumerate((g0, g1)):
        most = buf.at[pl.ds(0, n_inner - 1)]
        pltpu.make_async_copy(most, most, ag_send.at[n]).wait()
    pltpu.make_async_copy(core_out, core_out, core_send).wait()
    most = core_in.at[pl.ds(0, 28)]
    pltpu.make_async_copy(most, most, z_send).wait()


def body(a_vals, a_cols, b_vals, b_cols, c_cols, c_keep, c_vals):
    n_inner = NX * NY
    a = jnp.transpose(a_vals[0], (1, 0, 2)).reshape(6, 2, 8, 32, 128)
    a = jnp.transpose(a, (0, 1, 3, 2, 4)).reshape(6, 2, 256, 128)
    b = jnp.transpose(b_vals[0].reshape(4, 32, 128), (1, 0, 2)).reshape(128, 128)
    acol = jnp.transpose(a_cols, (2, 0, 1))
    hbm = pl.BlockSpec(memory_space=pltpu.HBM)
    vmem, smem, dma = pltpu.VMEM, pltpu.SMEM, pltpu.SemaphoreType.DMA
    out = pl.pallas_call(
        kernel,
        out_shape=jax.ShapeDtypeStruct((16, 32, 128), F32),
        in_specs=[hbm] * 7,
        out_specs=pl.BlockSpec(memory_space=pltpu.VMEM),
        scratch_shapes=[
            vmem((6, 2, 256, 128), F32),
            vmem((6, 1, 16), I32),
            vmem((128, 128), F32),
            smem((1, 4), I32),
            vmem((16, 16), I32),
            smem((1, 16), I32),
            vmem((16, 32, 128), F32),
            vmem((n_inner, TOP + 8, 128), F32),
            vmem((n_inner, 128 - TOP, 128), F32),
            vmem((96, 64, 128), BF16),
            vmem((n_inner * 4 * CAP + 1, 32, 128), F32),
            vmem((n_inner, 128), I32),
            smem((n_inner, 128), I32),
            vmem((16, 128), I32),
            smem((16, 128), I32),
            vmem((32, 4, 32, 128), F32),
            vmem((32, 4, 32, 128), F32),
            vmem((32, 4, 32, 128), F32),
            dma((9,)),
            dma((2,)),
            dma((24,)),
            dma((40,)),
            dma,
            dma((32,)),
            dma,
            dma((28,)),
        ],
        compiler_params=pltpu.CompilerParams(
            collective_id=0, has_side_effects=True, vmem_limit_bytes=(64 << 20) - (64 << 10)
        ),
        cost_estimate=pl.CostEstimate(flops=1 << 31, bytes_accessed=8 << 20, transcendentals=0),
    )(a, acol, b, b_cols, c_cols, c_keep.T, c_vals.reshape(16, 32, 128))
    return out.reshape(16, 1, 4096)


def solution(mesh):
    in_specs = (
        P("layer", "blk", None, None),
        P("layer", "blk", None),
        P(("blk", "layer"), None, None),
        P(("blk", "layer"), None),
        P("blk", None),
        P("blk", "layer"),
        P("blk", "layer", None),
    )
    out_specs = P("blk", "layer", None)
    return jax.shard_map(body, mesh=mesh, in_specs=in_specs, out_specs=out_specs, check_vma=False)
```
